32 devices in a mesh: frame: 16 (over z, x, core), row: 2 (over y).
Axes of the slice: x: 2, y: 2, z: 4, core: 2. Of those that a mesh axis runs over, the one named last changes fastest.
Arguments:
- latents: bfloat16 [64, 32, 32, 320], P('frame', 'row'), may hold values from -20 to 20
- ln_gain: bfloat16 [320], replicated, may hold values from 0.099609375 to 1.8984375
- q_weight: bfloat16 [320, 320], replicated, may hold values from -0.30078125 to 0.30078125
- k_weight: bfloat16 [320, 320], replicated, may hold values from -3 to 3
- v_weight: bfloat16 [320, 320], replicated, may hold values from -0.3125 to 0.3125
- o_weight: bfloat16 [320, 320], replicated, may hold values from -0.3125 to 0.3125
- gn_gain: bfloat16 [320], replicated, may hold values from 0.099609375 to 1.8984375
- conv_weight: bfloat16 [3, 3, 320, 320], replicated, may hold values from -0.109375 to 0.109375
- conv_bias: bfloat16 [320], replicated, may hold values from -3 to 3
Outputs:
- output: bfloat16 [64, 32, 32, 320], P('frame', 'row')
The draws below stay inside these ranges and needn't reach their ends.
All inputs are finite; a program needn't handle non-finite values.
Results may differ from the reference program's by a relative error of at most 0.0085.
The reference program's roundings to bfloat16 on the way count: a program that leaves them out, or rounds other values in their place, can miss the bound.
Values may be sent and summed in bfloat16 or wider, within the bound.
No kernel may reach another device: no remote copies, remote signals or barrier semaphores. Data moves between devices by JAX's collectives and lax.ppermute only.
A program may use at most 128 MiB of HBM per device.

```python
import math
import jax
import jax.numpy as jnp
from jax import lax

D = 320
HEADS = 8
GROUPS = 32
ROWS = 32
COLS = 32
FRAMES = 64


weight_edge = 0.30078125


def draw_latents(key, part):
    full_shape = (FRAMES, ROWS, COLS, D)
    keys_list = jax.random.split(key, 3)
    ramp = jnp.arange(ROWS, dtype=jnp.float32) / max(ROWS - 1, 1)
    jitter = jax.random.uniform(keys_list[1], (FRAMES, ROWS, 1, 1), minval=-0.25, maxval=0.25)
    spread = jnp.exp(math.log(3.0) * ramp[None, :, None, None] + jitter)
    rough = jnp.exp(jax.random.uniform(keys_list[2], (FRAMES, ROWS, COLS, 1), minval=-0.5, maxval=0.5))
    values = jax.random.normal(keys_list[0], full_shape) * spread * rough
    return jnp.clip(values, -20.0, 20.0).astype(jnp.bfloat16)


def shared_base(key):
    return jax.random.normal(jax.random.fold_in(key, 11), (D, D)) * math.sqrt(2.0 / D)


def draw_q_weight(key, part):
    return jnp.clip(shared_base(key), -weight_edge, weight_edge).astype(jnp.bfloat16)


def draw_k_weight(key, part):
    own_part = jax.random.normal(jax.random.fold_in(key, 12), (D, D)) * math.sqrt(2.0 / D)
    values = jnp.clip(own_part, -weight_edge, weight_edge)
    return values.astype(jnp.bfloat16)


def bell_draw(stream_key, dims, width, most, held_as=jnp.bfloat16):
    return jnp.clip(width * jax.random.normal(stream_key, dims, jnp.float32), -most, most).astype(held_as)


def setup_inputs(seed: int = 0) -> dict:
    streams_of = jax.random.split(jax.random.key(seed), 10)
    return {
        "latents": draw_latents(jax.random.fold_in(streams_of[9], 71), 0),
        "ln_gain": jnp.clip(1.0 + 0.18 * jax.random.normal(streams_of[1], (D,), jnp.float32), 0.099609375, 1.8984375).astype(jnp.bfloat16),
        "q_weight": draw_q_weight(jax.random.fold_in(streams_of[9], 71), 0),
        "k_weight": draw_k_weight(jax.random.fold_in(streams_of[9], 71), 0),
        "v_weight": bell_draw(streams_of[4], (D, D), D ** -0.5, 0.3125),
        "o_weight": bell_draw(streams_of[5], (D, D), D ** -0.5, 0.3125),
        "gn_gain": jnp.clip(1.0 + 0.18 * jax.random.normal(streams_of[6], (D,), jnp.float32), 0.099609375, 1.8984375).astype(jnp.bfloat16),
        "conv_weight": bell_draw(streams_of[7], (3, 3, D, D), (9 * D) ** -0.5, 0.109375),
        "conv_bias": bell_draw(streams_of[8], (D,), 0.5, 3.0),
    }


def layer_normed(values, gain_vec):
    floated = values.astype(jnp.float32)
    centre = floated - lax.optimization_barrier(jnp.mean(floated, axis=-1, keepdims=True))
    spread = lax.optimization_barrier(jnp.mean(centre * centre, axis=-1, keepdims=True))
    return (centre * lax.rsqrt(spread + 1e-05) * gain_vec.astype(jnp.float32)).astype(jnp.bfloat16)

def reference(latents, ln_gain, q_weight, k_weight, v_weight, o_weight, gn_gain, conv_weight, conv_bias):
    frame_tokens = ROWS * COLS
    head_dim = D // HEADS
    factor = 1.0 / math.sqrt(head_dim)
    tokens = latents.reshape(FRAMES * frame_tokens, D)
    normed = layer_normed(tokens, ln_gain)
    queries = jnp.dot(normed, q_weight, preferred_element_type=jnp.float32).astype(jnp.bfloat16)
    key_rows = jnp.dot(normed, k_weight, preferred_element_type=jnp.float32).astype(jnp.bfloat16)
    value_rows = jnp.dot(normed, v_weight, preferred_element_type=jnp.float32).astype(jnp.bfloat16)
    queries, key_rows, value_rows = lax.optimization_barrier((queries, key_rows, value_rows))
    four_shape = (FRAMES, frame_tokens, HEADS, head_dim)
    queries = queries.reshape(four_shape)
    key_rows = key_rows.reshape(four_shape)
    value_rows = value_rows.reshape(four_shape)
    earlier = jnp.maximum(jnp.arange(FRAMES, dtype=jnp.int32) - 1, 0)

    def single(index):
        frame_queries = queries[index].astype(jnp.float32)
        all_keys = jnp.concatenate([key_rows[0], key_rows[earlier[index]]], axis=0).astype(jnp.float32)
        all_values = jnp.concatenate([value_rows[0], value_rows[earlier[index]]], axis=0).astype(jnp.float32)
        scores = jnp.einsum('qhd,khd->hqk', frame_queries, all_keys) * factor
        highest = lax.optimization_barrier(jnp.max(scores, axis=-1, keepdims=True))
        raised = jnp.exp(scores - highest)
        totals = lax.optimization_barrier(jnp.sum(raised, axis=-1))
        weights = lax.optimization_barrier(raised.astype(jnp.bfloat16)).astype(jnp.float32)
        summed = jnp.einsum('hqk,khd->qhd', weights, all_values)
        return (summed / jnp.transpose(totals)[:, :, None]).astype(jnp.bfloat16)
    attended = lax.map(single, jnp.arange(FRAMES, dtype=jnp.int32)).reshape(FRAMES * frame_tokens, D)
    mixed = jnp.dot(attended, o_weight, preferred_element_type=jnp.float32)
    updated = (tokens.astype(jnp.float32) + mixed).astype(jnp.bfloat16)
    group_width = D // GROUPS
    grouped = updated.astype(jnp.float32).reshape(FRAMES, frame_tokens, GROUPS, group_width)
    counted = frame_tokens * group_width
    group_mean = lax.optimization_barrier(jnp.sum(grouped, axis=(1, 3))) / counted
    group_var = lax.optimization_barrier(jnp.sum(grouped * grouped, axis=(1, 3))) / counted - group_mean * group_mean
    scaled = (grouped - group_mean[:, None, :, None]) * lax.rsqrt(group_var + 1e-05)[:, None, :, None]
    activated = jax.nn.silu(scaled.reshape(FRAMES, frame_tokens, D) * gn_gain.astype(jnp.float32))
    activated = activated.astype(jnp.bfloat16).reshape(FRAMES, ROWS, COLS, D)
    padded = jnp.pad(activated, ((0, 0), (1, 1), (1, 1), (0, 0)))
    convolved = jnp.zeros((FRAMES * frame_tokens, D), jnp.float32)
    for row_off in range(3):
        for col_off in range(3):
            window = padded[:, row_off:row_off + ROWS, col_off:col_off + COLS, :].reshape(FRAMES * frame_tokens, D)
            convolved = convolved + jnp.dot(window, conv_weight[row_off, col_off], preferred_element_type=jnp.float32)
    output = updated.astype(jnp.float32) + convolved + conv_bias.astype(jnp.float32)
    return output.astype(jnp.bfloat16).reshape(FRAMES, ROWS, COLS, D)
```

```python
import functools
import math

import jax
import jax.numpy as jnp
import numpy as np
from jax import lax
from jax.experimental import pallas as pl
from jax.experimental.pallas import tpu as pltpu
from jax.sharding import PartitionSpec as P

HEADS = 8
GROUPS = 32
KPAD = 64
VPAD = 48
BF16, F32 = jnp.bfloat16, jnp.float32
VMEM_BYTES = 50 * 2**20


def head_spread(channels, pad):
    dim = channels // HEADS
    out = np.zeros((HEADS * pad, channels), np.float32)
    for c in range(channels):
        out[c // dim * pad + c % dim, c] = 1.0
    return jnp.asarray(out, BF16)


def nt(a, b):
    return lax.dot_general(a, b, (((1,), (1,)), ((), ())), preferred_element_type=F32)


def normed_of(x, gain):
    floated = x.astype(F32)
    centre = floated - jnp.mean(floated, axis=-1, keepdims=True)
    spread = jnp.mean(centre * centre, axis=-1, keepdims=True)
    return (centre * lax.rsqrt(spread + 1e-05) * gain).astype(BF16)


def params(grid_rank=1):
    return pltpu.CompilerParams(
        vmem_limit_bytes=VMEM_BYTES, dimension_semantics=("arbitrary",) * grid_rank
    )


def query_kernel(x_ref, g_ref, wq_ref, wk_ref, wv_ref, wo_ref, ek_ref, ev_ref,
                 qt_ref, wkp_ref, wvt_ref, wop_ref, wqt_ref):
    @pl.when(pl.program_id(0) == 0)
    def _():
        ek, ev = ek_ref[...], ev_ref[...]
        wqt_ref[...] = nt(ek, wq_ref[...]).astype(BF16)
        wkp_ref[...] = nt(wk_ref[...], ek).astype(BF16)
        wvt_ref[...] = nt(ev, wv_ref[...]).astype(BF16)
        wop_ref[...] = jnp.dot(ev, wo_ref[...], preferred_element_type=F32).astype(BF16)

    normed = normed_of(x_ref[0], g_ref[...].astype(F32))
    qt_ref[0] = nt(wqt_ref[...], normed).astype(BF16)


def make_queries(x, gain, wq, wk, wv, wo):
    frames, tok, ch = x.shape
    ek, ev = head_spread(ch, KPAD), head_spread(ch, VPAD)
    nk, nv = HEADS * KPAD, HEADS * VPAD
    whole = lambda shape: pl.BlockSpec(shape, lambda i: (0,) * len(shape))
    return pl.pallas_call(
        query_kernel,
        grid=(frames,),
        in_specs=[pl.BlockSpec((1, tok, ch), lambda i: (i, 0, 0)), whole((1, ch))]
        + [whole((ch, ch))] * 4 + [whole((nk, ch)), whole((nv, ch))],
        out_specs=[pl.BlockSpec((1, nk, tok), lambda i: (i, 0, 0)),
                   whole((ch, nk)), whole((nv, ch)), whole((nv, ch))],
        out_shape=[jax.ShapeDtypeStruct((frames, nk, tok), BF16),
                   jax.ShapeDtypeStruct((ch, nk), BF16),
                   jax.ShapeDtypeStruct((nv, ch), BF16),
                   jax.ShapeDtypeStruct((nv, ch), BF16)],
        scratch_shapes=[pltpu.VMEM((nk, ch), BF16)],
        compiler_params=params(),
        cost_estimate=pl.CostEstimate(flops=3_000_000_000, bytes_accessed=6_000_000, transcendentals=0),
        name="queries",
    )(x, gain, wq, wk, wv, wo, ek, ev)


def flash_kernel(cfg, *refs):
    segs, once, first, last, select, rows, pair = cfg
    refs = list(refs)
    take = lambda n: [refs.pop(0) for _ in range(n)]
    (flag_ref,) = take(1)
    seg_refs = take(segs * (2 if select else 1))
    qt_ref, g_ref, wkp_ref, wvt_ref = take(4)
    if not first:
        m_in, acc_in = take(2)
    if last:
        x_ref, wop_ref = take(2)
        upd_ref, edge_ref, stat_ref = take(3)
    else:
        m_out, acc_out = take(2)
    k_ref, vt_ref, s_ref = take(3)
    att_ref = refs.pop(0) if last else None
    tok = qt_ref.shape[2]
    ch = g_ref.shape[1]
    dim = ch // HEADS
    factor = math.log2(math.e) / math.sqrt(dim)

    def make_kv():
        at = 0
        gain = g_ref[...].astype(F32)
        for i in range(segs):
            x = seg_refs[i][0]
            if select:
                x = jnp.where(flag_ref[0] == 0, seg_refs[segs + i][0], x)
            n = x.shape[0]
            normed = normed_of(x, gain)
            k_ref[at:at + n, :] = jnp.dot(normed, wkp_ref[...], preferred_element_type=F32).astype(BF16)
            vt = nt(wvt_ref[...], normed).astype(BF16)
            for h in range(HEADS):
                vt_ref[h * VPAD:(h + 1) * VPAD, at:at + n] = vt[h * VPAD:(h + 1) * VPAD]
            at += n

    if once:
        pl.when(pl.program_id(0) == 0)(make_kv)
    else:
        make_kv()

    zeros = jnp.zeros((KPAD, tok), BF16)
    row = lax.broadcasted_iota(jnp.int32, (VPAD, vt_ref.shape[1]), 0)

    def scores(h):
        own = qt_ref[0, h * KPAD:(h + 1) * KPAD, :]
        both = jnp.concatenate([own, zeros] if h % 2 == 0 else [zeros, own], axis=0)
        lanes = h // 2 * 2 * KPAD
        s_ref[h % 2] = jnp.dot(k_ref[:, lanes:lanes + 2 * KPAD], both, preferred_element_type=F32)

    scores(0)
    for h in range(HEADS):
        if h + 1 < HEADS:
            scores(h + 1)
        s = s_ref[h % 2]
        top = jnp.max(s, axis=0, keepdims=True)
        if not first:
            old = m_in[0, h:h + 1, :]
            top = jnp.maximum(top, old)
        weights = jnp.exp2((s - top) * factor).astype(BF16)
        values = vt_ref[h * VPAD:(h + 1) * VPAD, :]
        values = jnp.where(row == dim, jnp.ones_like(values), values)
        part = jnp.dot(values, weights, preferred_element_type=F32)
        if not first:
            part = part + acc_in[0, h * VPAD:(h + 1) * VPAD, :] * jnp.exp2((old - top) * factor)
        if last:
            att_ref[h * VPAD:(h + 1) * VPAD, :] = (part / part[dim:dim + 1]).astype(BF16)
        else:
            m_out[0, h:h + 1, :] = top
            acc_out[0, h * VPAD:(h + 1) * VPAD, :] = part

    if last:
        mixed = lax.dot_general(att_ref[...], wop_ref[...], (((0,), (0,)), ((), ())),
                                preferred_element_type=F32)
        updated = (x_ref[0].astype(F32) + mixed).astype(BF16)
        upd_ref[0] = updated
        floated = updated.astype(F32)
        cols = tok // rows
        sums = jnp.sum(floated, axis=0, keepdims=True)
        squares = jnp.sum(floated * floated, axis=0, keepdims=True)
        which = lax.broadcasted_iota(jnp.int32, (8, ch), 0)
        stats = jnp.where(which == 0, sums, jnp.where(which == 1, squares, 0.0))
        stat_ref[0] = stats
        if pair:
            edge_ref[0, 0:cols] = jnp.where(flag_ref[1] == 0, floated[tok - cols:], floated[:cols])
            edge_ref[0, cols:cols + 8] = stats
        else:
            edge_ref[0, 0:cols] = floated[:cols]
            edge_ref[0, cols:2 * cols] = floated[tok - cols:]


def flash(name, flags, start, count, segments, qt, gain, wkp, wvt, state=None, once=False,
          select=None, last=None, rows=None, pair=True):
    frames, nk, tok = qt.shape
    ch = gain.shape[1]
    nv = HEADS * VPAD
    whole = lambda shape: pl.BlockSpec(shape, lambda i: (0,) * len(shape))
    seg_specs, seg_args = [], []
    for arr, block in list(segments) + list(select or []):
        seg_specs.append(pl.BlockSpec((1,) + arr.shape[1:], functools.partial(lambda b, i: (b(i), 0, 0), block)))
        seg_args.append(arr)
    keys = sum(arr.shape[1] for arr, _ in segments)
    frame = lambda shape: pl.BlockSpec((1,) + shape, lambda i: (i + start, 0, 0))
    first = state is None
    in_specs = [pl.BlockSpec(memory_space=pltpu.SMEM)] + seg_specs + [
        frame((nk, tok)), whole((1, ch)), whole(wkp.shape), whole(wvt.shape)]
    args = [flags] + seg_args + [qt, gain, wkp, wvt]
    aliases = {}
    state_shapes = [jax.ShapeDtypeStruct((frames, HEADS, tok), F32), jax.ShapeDtypeStruct((frames, nv, tok), F32)]
    state_specs = [frame((HEADS, tok)), frame((nv, tok))]
    scratch = [pltpu.VMEM((keys, nk), BF16), pltpu.VMEM((nv, keys), BF16), pltpu.VMEM((2, keys, tok), F32)]
    if not first:
        if last is None:
            aliases = {len(args): 0, len(args) + 1: 1}
        in_specs += state_specs
        args += list(state)
    if last is None:
        out_shape, out_specs = state_shapes, state_specs
    else:
        x, wop = last
        cols = tok // rows
        in_specs += [frame((tok, ch)), whole(wop.shape)]
        args += [x, wop]
        edge = cols + 8 if pair else 2 * cols
        out_shape = [jax.ShapeDtypeStruct((count, tok, ch), BF16),
                     jax.ShapeDtypeStruct((count, edge, ch), F32),
                     jax.ShapeDtypeStruct((count, 8, ch), F32)]
        out_specs = [pl.BlockSpec((1,) + o.shape[1:], lambda i: (i, 0, 0)) for o in out_shape]
        scratch.append(pltpu.VMEM((nv, tok), BF16))
    cfg = (len(segments), once, first, last is not None, select is not None, rows, pair)
    scores = count * HEADS * keys * tok
    return pl.pallas_call(
        functools.partial(flash_kernel, cfg),
        grid=(count,),
        in_specs=in_specs,
        out_specs=out_specs,
        out_shape=out_shape,
        scratch_shapes=scratch,
        input_output_aliases=aliases,
        compiler_params=params(),
        cost_estimate=pl.CostEstimate(flops=scores * 1400, bytes_accessed=scores // 8, transcendentals=scores),
        name=name,
    )(*args)


def conv_kernel(cfg, flag_ref, upd_ref, top_ref, bot_ref, stat_ref, gn_ref, bias_ref, group_ref, w_ref,
                out_ref, act_ref):
    rows, cols, count, pair, bot_at = cfg
    tok, ch = upd_ref.shape[1:]
    stats = stat_ref[0]
    if pair:
        stats = stats + top_ref[0, cols:cols + 8]
    grouped = jnp.dot(stats, group_ref[...].astype(F32), precision=lax.Precision.HIGHEST,
                      preferred_element_type=F32) / count
    mean = grouped[0:1]
    var = grouped[1:2] - mean * mean
    scale = lax.rsqrt(var + 1e-05)
    gain = gn_ref[...].astype(F32)

    def activated(u):
        v = (u.astype(F32) - mean) * scale * gain
        return v / (1.0 + jnp.exp(-v))

    above = jnp.where(flag_ref[2] == 1, activated(top_ref[0, 0:cols]), 0.0)
    below = jnp.where(flag_ref[3] == 1, activated(bot_ref[0, bot_at:bot_at + cols]), 0.0)
    act_ref[0:cols] = above.astype(BF16)
    act_ref[cols:cols + tok] = activated(upd_ref[0]).astype(BF16)
    act_ref[cols + tok:2 * cols + tok] = below.astype(BF16)
    column = lax.broadcasted_iota(jnp.int32, (tok, ch), 0) % cols
    total = upd_ref[0].astype(F32) + bias_ref[...].astype(F32)
    for b in range(3):
        part = jnp.zeros((tok, ch), F32)
        for a in range(3):
            part += jnp.dot(act_ref[a * cols:a * cols + tok, :], w_ref[a, b], preferred_element_type=F32)
        if b == 0:
            part = jnp.where(column == 0, 0.0, pltpu.roll(part, 1, 0))
        if b == 2:
            part = jnp.where(column == cols - 1, 0.0, pltpu.roll(part, tok - 1, 0))
        total += part
    out_ref[0] = total.astype(BF16)


def conv(flags, upd, top, bot, bot_at, stats, gn, bias, group, weight, rows, pair, count):
    frames, tok, ch = upd.shape
    cols = tok // rows
    per = lambda a: pl.BlockSpec((1,) + a.shape[1:], lambda i: (i, 0, 0))
    whole = lambda a: pl.BlockSpec(a.shape, lambda i: (0,) * a.ndim)
    return pl.pallas_call(
        functools.partial(conv_kernel, (rows, cols, count, pair, bot_at)),
        grid=(frames,),
        in_specs=[pl.BlockSpec(memory_space=pltpu.SMEM), per(upd), per(top), per(bot), per(stats),
                  whole(gn), whole(bias), whole(group), whole(weight)],
        out_specs=per(upd),
        out_shape=jax.ShapeDtypeStruct(upd.shape, BF16),
        scratch_shapes=[pltpu.VMEM((tok + 2 * cols, ch), BF16)],
        compiler_params=params(),
        cost_estimate=pl.CostEstimate(flops=frames * tok * ch * ch * 40, bytes_accessed=4_000_000, transcendentals=0),
        name="conv",
    )(flags, upd, top, bot, stats, gn, bias, group, weight)


def spread_first(value, axis):
    size = lax.axis_size(axis)
    me = lax.axis_index(axis)
    stride = 1
    while stride * 2 < size:
        stride *= 2
    have = [0]
    while stride >= 1:
        route = [(i, i + stride) for i in have if i + stride < size]
        if route:
            got = lax.ppermute(value, axis, route)
            new = [j for _, j in route]
            value = jnp.where((me % (2 * stride)) == stride, got, value)
            have += new
        stride //= 2
    return value


def others(value, rows, axis=1):
    got = [lax.ppermute(value, "row", [(i, (i + k) % rows) for i in range(rows)]) for k in range(1, rows)]
    return got[0] if len(got) == 1 else jnp.concatenate(got, axis=axis)


def body(latents, ln_gain, q_weight, k_weight, v_weight, o_weight, gn_gain, conv_weight, conv_bias):
    frames, row_count, cols, ch = latents.shape
    tok = row_count * cols
    size, blocks = lax.axis_size("row"), lax.axis_size("frame")
    me, block = lax.axis_index("row"), lax.axis_index("frame")
    pair = size == 2
    x = latents.reshape(frames, tok, ch)
    gain = ln_gain.reshape(1, ch)
    flags = jnp.stack([block, me, (me > 0).astype(jnp.int32), (me < size - 1).astype(jnp.int32)]).astype(jnp.int32)

    last_own = x[frames - 1:]
    routes = [[(f * size + r, (f + 1) * size + (r + k) % size) for f in range(blocks - 1) for r in range(size)]
              for k in range(size)]
    lead = spread_first(x[0:1], "frame")
    side = others(x[0:frames - 1], size)
    came = [lax.ppermute(last_own, ("frame", "row"), route) for route in routes]
    prev_own = came[0]
    prev_side = came[1] if size == 2 else jnp.concatenate(came[1:], axis=1)
    lead_side = others(lead, size)

    qt, wkp, wvt, wop = make_queries(x, gain, q_weight, k_weight, v_weight, o_weight)
    common = (qt, gain, wkp, wvt)
    state = flash("own", flags, 1, frames - 1, [(x, lambda i: i)], *common)
    state = flash("side", flags, 1, frames - 1, [(side, lambda i: i)], *common, state=state)
    zero = lambda i: 0
    state0 = flash("prev", flags, 0, 1, [(prev_own, zero), (prev_side, zero)], *common,
                   select=[(x, zero), (side, zero)])
    state = [lax.dynamic_update_slice_in_dim(s, s0[0:1], 0, 0) for s, s0 in zip(state, state0)]
    half = frames // 2
    group = jnp.asarray(np.kron(np.eye(GROUPS), np.ones((ch // GROUPS,) * 2)), BF16)
    outs = []
    for start in (0, half):
        upd, edge, stats = flash("lead", flags, start, half, [(lead, zero), (lead_side, zero)], *common,
                                 state=state, once=True, last=(x, wop), rows=row_count, pair=pair)
        if pair:
            got = lax.ppermute(edge, "row", [(0, 1), (1, 0)])
            top, bot, bot_at = got, got, 0
        else:
            top = lax.ppermute(edge[:, cols:], "row", [(i, i + 1) for i in range(size - 1)])
            bot = lax.ppermute(edge[:, :cols], "row", [(i + 1, i) for i in range(size - 1)])
            bot_at = 0
            stats = lax.psum(stats, "row")
        outs.append(conv(flags, upd, top, bot, bot_at, stats, gn_gain.reshape(1, ch), conv_bias.reshape(1, ch),
                         group, conv_weight, row_count, pair, tok * size * (ch // GROUPS)))
    return jnp.concatenate(outs, axis=0).reshape(latents.shape)


def solution(mesh):
    in_specs = (P("frame", "row", None, None), P(), P(), P(), P(), P(), P(), P(), P())
    out_specs = P("frame", "row", None, None)
    return jax.shard_map(body, mesh=mesh, in_specs=in_specs, out_specs=out_specs, check_vma=False)
```

```python
import functools
import math

import jax
import jax.numpy as jnp
from jax import lax
from jax.experimental import pallas as pl
from jax.experimental.pallas import tpu as pltpu
from jax.sharding import PartitionSpec as P

HEADS = 8
GROUPS = 32
KPAD = 64
VPAD = 48
BF16, F32, I32 = jnp.bfloat16, jnp.float32, jnp.int32
VMEM_BYTES = 28 * 2**20


def nt(a, b):
    return lax.dot_general(a, b, (((1,), (1,)), ((), ())), preferred_element_type=F32)


def params():
    return pltpu.CompilerParams(vmem_limit_bytes=VMEM_BYTES, dimension_semantics=("arbitrary",))


def cost(flops, moved, exps=0):
    return pl.CostEstimate(flops=int(flops), bytes_accessed=int(moved), transcendentals=int(exps))


def whole(a):
    return pl.BlockSpec(a.shape, lambda i: (0,) * len(a.shape))


def blocked(a, index):
    return pl.BlockSpec((1,) + a.shape[1:], lambda i: (index(i),) + (0,) * (len(a.shape) - 1))


def shape_of(*dims, dtype=BF16):
    return jax.ShapeDtypeStruct(dims, dtype)


def head_spread(channels, pad):
    dim = channels // HEADS
    shape = (HEADS * pad, channels)
    row = lax.broadcasted_iota(I32, shape, 0)
    col = lax.broadcasted_iota(I32, shape, 1)
    head = sum((row >= h * pad).astype(I32) for h in range(1, HEADS))
    inside = row - head * pad
    return jnp.where((inside < dim) & (head * dim + inside == col), 1.0, 0.0).astype(BF16)


def project_kernel(x_ref, g_ref, wq_ref, wk_ref, wv_ref, wo_ref,
                   qt_ref, main_ref, first_ref, last_ref, wkp_ref, wvt_ref, wop_ref, wqt_ref):
    i, n = pl.program_id(0), pl.num_programs(0)
    ch = g_ref.shape[1]

    @pl.when(i == 0)
    def _():
        ek, ev = head_spread(ch, KPAD), head_spread(ch, VPAD)
        wqt_ref[...] = nt(ek, wq_ref[...]).astype(BF16)
        wkp_ref[...] = nt(wk_ref[...], ek).astype(BF16)
        wvt_ref[...] = nt(ev, wv_ref[...]).astype(BF16)
        wop_ref[...] = jnp.dot(ev, wo_ref[...], preferred_element_type=F32).astype(BF16)

    floated = x_ref[0].astype(F32)
    centre = floated - jnp.mean(floated, axis=-1, keepdims=True)
    spread = jnp.mean(centre * centre, axis=-1, keepdims=True)
    normed = (centre * lax.rsqrt(spread + 1e-05) * g_ref[...].astype(F32)).astype(BF16)

    @pl.when(i < n - 1)
    def _():
        main_ref[0] = normed

    @pl.when(i == 0)
    def _():
        first_ref[0] = normed

    @pl.when(i == n - 1)
    def _():
        last_ref[0] = normed

    qt_ref[0] = nt(wqt_ref[...], normed).astype(BF16)


def project(x, gain, wq, wk, wv, wo):
    frames, tok, ch = x.shape
    nk, nv = HEADS * KPAD, HEADS * VPAD
    outs = [shape_of(frames, nk, tok), shape_of(frames - 1, tok, ch), shape_of(1, tok, ch), shape_of(1, tok, ch),
            shape_of(ch, nk), shape_of(nv, ch), shape_of(nv, ch)]
    each = lambda i: i
    return pl.pallas_call(
        project_kernel,
        grid=(frames,),
        in_specs=[blocked(x, each)] + [whole(a) for a in (gain, wq, wk, wv, wo)],
        out_specs=[blocked(outs[0], each), blocked(outs[1], lambda i: jnp.minimum(i, frames - 2))]
        + [whole(o) for o in outs[2:]],
        out_shape=outs,
        scratch_shapes=[pltpu.VMEM((nk, ch), BF16)],
        compiler_params=params(),
        cost_estimate=cost(frames * tok * ch * nk * 8, 8e6),
        name="project",
    )(x, gain, wq, wk, wv, wo)


def flash_kernel(cfg, *refs):
    late, first, last, rows, pair = cfg
    refs = list(refs)
    take = lambda n: [refs.pop(0) for _ in range(n)]
    seg_ref, segn_ref = take(2)
    late_ref = refs.pop(0) if late else None
    qt_ref, qtn_ref, wkp_ref, wvt_ref = take(4)
    if not first:
        m_in, acc_in = take(2)
    if last:
        x_ref, wop_ref, upd_ref, edge_ref, stat_ref = take(5)
    else:
        m_out, acc_out = take(2)
    k_ref, vt_ref, s_ref = take(3)
    if last:
        att_ref = refs.pop(0)
    i, n = pl.program_id(0), pl.num_programs(0)
    tok, ch = qt_ref.shape[2], wkp_ref.shape[0]
    keys = seg_ref.shape[1]
    dim = ch // HEADS
    factor = math.log2(math.e) / math.sqrt(dim)
    once = not late
    zeros = jnp.zeros((KPAD, tok), BF16)
    ones_row = lax.broadcasted_iota(I32, (16, keys), 0) == dim % 16

    def make_keys(seg):
        k_ref[...] = jnp.dot(seg, wkp_ref[...], preferred_element_type=F32).astype(BF16)

    def make_values(seg):
        vt = nt(wvt_ref[...], seg).astype(BF16)
        for h in range(HEADS):
            at = h * VPAD + dim // 16 * 16
            vt_ref[h * VPAD:at] = vt[h * VPAD:at]
            vt_ref[at:at + 16] = jnp.where(ones_row, jnp.ones((16, keys), BF16), vt[at:at + 16])
            if at + 16 < (h + 1) * VPAD:
                vt_ref[at + 16:(h + 1) * VPAD] = vt[at + 16:(h + 1) * VPAD]

    def scores(q_ref, h):
        own = q_ref[0, h * KPAD:(h + 1) * KPAD, :]
        both = jnp.concatenate([own, zeros] if h % 2 == 0 else [zeros, own], axis=0)
        lanes = h // 2 * 2 * KPAD
        s_ref[h % 2] = jnp.dot(k_ref[:, lanes:lanes + 2 * KPAD], both, preferred_element_type=F32)

    @pl.when(i == 0)
    def _():
        seg = seg_ref[0]
        make_keys(seg)
        make_values(seg)
        scores(qt_ref, 0)

    if not once:
        segn = segn_ref[0]
        use_late = (i >= n - 2) & (lax.axis_index("frame") > 0)
        segn = jnp.where(use_late, late_ref[0], segn)

    for h in range(HEADS):
        top = jnp.max(s_ref[h % 2], axis=0, keepdims=True)
        if h + 1 < HEADS:
            scores(qt_ref, h + 1)
        else:
            if not once:
                make_keys(segn)
            scores(qtn_ref, 0)
        if not first:
            old = m_in[0, h:h + 1, :]
            top = jnp.maximum(top, old)
        weights = jnp.exp2((s_ref[h % 2] - top) * factor).astype(BF16)
        part = jnp.dot(vt_ref[h * VPAD:(h + 1) * VPAD, :], weights, preferred_element_type=F32)
        if not first:
            part = part + acc_in[0, h * VPAD:(h + 1) * VPAD, :] * jnp.exp2((old - top) * factor)
        if last:
            att_ref[h * VPAD:(h + 1) * VPAD, :] = (part / part[dim:dim + 1]).astype(BF16)
        else:
            m_out[0, h:h + 1, :] = top
            acc_out[0, h * VPAD:(h + 1) * VPAD, :] = part
    if not once:
        make_values(segn)

    if last:
        mixed = lax.dot_general(att_ref[...], wop_ref[...], (((0,), (0,)), ((), ())),
                                preferred_element_type=F32)
        updated = (x_ref[0].astype(F32) + mixed).astype(BF16)
        upd_ref[0] = updated
        floated = updated.astype(F32)
        cols = tok // rows
        sums = jnp.sum(floated, axis=0, keepdims=True)
        squares = jnp.sum(floated * floated, axis=0, keepdims=True)
        which = lax.broadcasted_iota(I32, (8, ch), 0)
        stats = jnp.where(which == 0, sums, jnp.where(which == 1, squares, 0.0))
        stat_ref[0] = stats
        if pair:
            edge_ref[0, 0:cols] = jnp.where(lax.axis_index("row") == 0, floated[tok - cols:], floated[:cols])
            edge_ref[0, cols:cols + 8] = stats
        else:
            edge_ref[0, 0:cols] = floated[:cols]
            edge_ref[0, cols:2 * cols] = floated[tok - cols:]


def flash(name, frame_of, count, seg, seg_of, qt, wkp, wvt, late=None, state=None, last=None, rows=None, pair=True):
    frames, nk, tok = qt.shape
    ch, nv, keys = wkp.shape[0], wvt.shape[0], seg.shape[1]
    after = lambda i: jnp.minimum(i + 1, count - 1)
    first = state is None
    in_specs = [blocked(seg, seg_of), blocked(seg, lambda i: seg_of(after(i)))]
    args = [seg, seg]
    if late is not None:
        in_specs.append(whole(late))
        args.append(late)
    in_specs += [blocked(qt, frame_of), pl.BlockSpec((1, KPAD, tok), lambda i: (frame_of(after(i)), 0, 0)),
                 whole(wkp), whole(wvt)]
    args += [qt, qt, wkp, wvt]
    state_shapes = [shape_of(frames, HEADS, tok, dtype=F32), shape_of(frames, nv, tok, dtype=F32)]
    state_specs = [blocked(s, frame_of) for s in state_shapes]
    aliases = {}
    scratch = [pltpu.VMEM((keys, nk), BF16), pltpu.VMEM((nv, keys), BF16), pltpu.VMEM((2, keys, tok), F32)]
    if not first:
        if last is None:
            aliases = {len(args): 0, len(args) + 1: 1}
        in_specs += state_specs
        args += list(state)
    if last is None:
        out_shape, out_specs = state_shapes, state_specs
    else:
        x, wop = last
        cols = tok // rows
        in_specs += [blocked(x, frame_of), whole(wop)]
        args += [x, wop]
        out_shape = [shape_of(count, tok, ch), shape_of(count, cols + 8 if pair else 2 * cols, ch, dtype=F32),
                     shape_of(count, 8, ch, dtype=F32)]
        out_specs = [blocked(o, lambda i: i) for o in out_shape]
        scratch.append(pltpu.VMEM((nv, tok), BF16))
    made = count * HEADS * keys * tok
    return pl.pallas_call(
        functools.partial(flash_kernel, (late is not None, first, last is not None, rows, pair)),
        grid=(count,),
        in_specs=in_specs,
        out_specs=out_specs,
        out_shape=out_shape,
        scratch_shapes=scratch,
        input_output_aliases=aliases,
        compiler_params=params(),
        cost_estimate=cost(made * 1400, made // 8, made),
        name=name,
    )(*args)


def conv_kernel(cfg, *refs):
    rows, cols, counted, pair, fresh = cfg
    refs = list(refs)
    take = lambda n: [refs.pop(0) for _ in range(n)]
    upd_ref, top_ref, bot_ref, stat_ref, gn_ref, bias_ref, w_ref = take(7)
    if not fresh:
        refs.pop(0)
    out_ref = refs.pop(0)
    if fresh:
        wide_ref = refs.pop(0)
    (act_ref,) = take(1)
    tok, ch = upd_ref.shape[1:]

    if fresh:
        @pl.when(pl.program_id(0) == 0)
        def _():
            for a in range(3):
                for b in range(3):
                    wide_ref[a * ch:(a + 1) * ch, b * ch:(b + 1) * ch] = w_ref[a, b]
    else:
        wide_ref = w_ref

    stats = stat_ref[0]
    if pair:
        stats = stats + top_ref[0, cols:cols + 8]
    width = ch // GROUPS
    lane = lax.broadcasted_iota(I32, (ch, GROUPS), 0)
    group = lax.broadcasted_iota(I32, (ch, GROUPS), 1)
    member = jnp.where((lane >= group * width) & (lane < (group + 1) * width), 1.0, 0.0)
    exact = functools.partial(lax.dot_general, precision=lax.Precision.HIGHEST, preferred_element_type=F32)
    grouped = exact(stats, member, (((1,), (0,)), ((), ()))) / counted
    mean = grouped[0:1]
    scale = lax.rsqrt(grouped[1:2] - mean * mean + 1e-05)
    which = lax.broadcasted_iota(I32, (8, GROUPS), 0)
    spread = exact(jnp.where(which == 0, mean, jnp.where(which == 1, scale, 0.0)), member, (((1,), (1,)), ((), ())))
    mean, scale = spread[0:1], spread[1:2] * gn_ref[...].astype(F32)

    def activated(u):
        v = (u.astype(F32) - mean) * scale
        return (v / (1.0 + jnp.exp(-v))).astype(BF16)

    me = lax.axis_index("row")
    above = jnp.where(me > 0, activated(top_ref[0, 0:cols]), jnp.zeros((cols, ch), BF16))
    below = jnp.where(me < lax.axis_size("row") - 1, activated(bot_ref[0, 0:cols]), jnp.zeros((cols, ch), BF16))
    middle = activated(upd_ref[0])
    act_ref[:, ch:2 * ch] = middle
    act_ref[0:cols, 0:ch] = above
    act_ref[cols:tok, 0:ch] = middle[0:tok - cols]
    act_ref[0:tok - cols, 2 * ch:] = middle[cols:tok]
    act_ref[tok - cols:tok, 2 * ch:] = below
    parts = jnp.dot(act_ref[...], wide_ref[...], preferred_element_type=F32)
    column = lax.broadcasted_iota(I32, (tok, ch), 0) % cols
    left = jnp.where(column == 0, 0.0, pltpu.roll(parts[:, 0:ch], 1, 0))
    right = jnp.where(column == cols - 1, 0.0, pltpu.roll(parts[:, 2 * ch:], tok - 1, 0))
    total = upd_ref[0].astype(F32) + (left + parts[:, ch:2 * ch] + right) + bias_ref[...].astype(F32)
    out_ref[0] = total.astype(BF16)


def conv(start, frames, upd, top, bot, stats, gn, bias, weight, rows, pair, counted, into=None):
    count, tok, ch = upd.shape
    cols = tok // rows
    each = lambda i: i
    result, wide = shape_of(frames, tok, ch), shape_of(3 * ch, 3 * ch)
    fresh = into is None
    args = [upd, top, bot, stats, gn, bias, weight if fresh else into[1]]
    in_specs = [blocked(a, each) for a in args[:4]] + [whole(a) for a in args[4:]]
    out_shape, out_specs = [result], [blocked(result, lambda i: i + start)]
    if fresh:
        out_shape.append(wide)
        out_specs.append(whole(wide))
    else:
        args.append(into[0])
        in_specs.append(pl.BlockSpec(memory_space=pl.ANY))
    return pl.pallas_call(
        functools.partial(conv_kernel, (rows, cols, counted, pair, fresh)),
        grid=(count,),
        in_specs=in_specs,
        out_specs=out_specs,
        out_shape=out_shape,
        scratch_shapes=[pltpu.VMEM((tok, 3 * ch), BF16)],
        input_output_aliases={} if fresh else {len(args) - 1: 0},
        compiler_params=params(),
        cost_estimate=cost(count * tok * ch * ch * 30, 4e6),
        name="conv",
    )(*args)


def spread_first(value, axis):
    size = lax.axis_size(axis)
    me = lax.axis_index(axis)
    stride = 1
    while stride * 2 < size:
        stride *= 2
    have = [0]
    while stride >= 1:
        new = [i + stride for i in have if i + stride < size]
        if new:
            got = lax.ppermute(value, axis, [(j - stride, j) for j in new])
            value = jnp.where((me & (2 * stride - 1)) == stride, got, value)
            have += new
        stride //= 2
    return value


def others(value, rows):
    got = [lax.ppermute(value, "row", [(i, (i + k) % rows) for i in range(rows)]) for k in range(1, rows)]
    return got[0] if len(got) == 1 else jnp.concatenate(got, axis=1)


def body(latents, ln_gain, q_weight, k_weight, v_weight, o_weight, gn_gain, conv_weight, conv_bias):
    frames, row_count, cols, ch = latents.shape
    tok = row_count * cols
    size, blocks = lax.axis_size("row"), lax.axis_size("frame")
    pair = size == 2
    x = latents.reshape(frames, tok, ch)
    line = lambda v: v.reshape(1, ch)

    qt, main, lead, tail, wkp, wvt, wop = project(x, line(ln_gain), q_weight, k_weight, v_weight, o_weight)
    routes = [[(f * size + r, (f + 1) * size + (r + k) % size) for f in range(blocks - 1) for r in range(size)]
              for k in range(size)]
    came = [lax.ppermute(tail, ("frame", "row"), route) for route in routes]
    prev_side = came[1] if pair else jnp.concatenate(came[1:], axis=1)
    side = others(main, size)
    lead = spread_first(lead, "frame")
    lead_side = others(lead, size)

    common = (qt, wkp, wvt)
    turned = lambda i: lax.rem(i + 1, frames)
    inner = lambda i: lax.rem(i, frames - 1)
    zero = lambda i: 0
    state = flash("own", turned, frames, main, inner, *common, late=came[0])
    state = flash("side", turned, frames, side, inner, *common, late=prev_side, state=state)
    state = flash("lead", lambda i: i, frames, lead, zero, *common, state=state)
    half = frames // 2
    into = None
    finished = []
    for start, count in ((0, half), (half, frames - half)):
        upd, edge, stats = flash("finish", lambda i: i + start, count, lead_side, zero, *common, state=state,
                                 last=(x, wop), rows=row_count, pair=pair)
        if pair:
            top = bot = lax.ppermute(edge, "row", [(0, 1), (1, 0)])
        else:
            top = lax.ppermute(edge[:, cols:], "row", [(i, i + 1) for i in range(size - 1)])
            bot = lax.ppermute(edge[:, :cols], "row", [(i + 1, i) for i in range(size - 1)])
            stats = lax.psum(stats, "row")
        finished.append((start, upd, top, bot, stats))
    for start, upd, top, bot, stats in finished:
        got = conv(start, frames, upd, top, bot, stats, line(gn_gain), line(conv_bias), conv_weight,
                   row_count, pair, tok * size * (ch // GROUPS), into)
        into = (got[0], got[1] if into is None else into[1])
    return into[0].reshape(latents.shape)


def solution(mesh):
    in_specs = (P("frame", "row", None, None), P(), P(), P(), P(), P(), P(), P(), P())
    out_specs = P("frame", "row", None, None)
    return jax.shard_map(body, mesh=mesh, in_specs=in_specs, out_specs=out_specs, check_vma=False)
```

```python
import functools
import math

import jax
import jax.numpy as jnp
from jax import lax
from jax.experimental import pallas as pl
from jax.experimental.pallas import tpu as pltpu
from jax.sharding import PartitionSpec as P

HEADS = 8
GROUPS = 32
KPAD = 64
VPAD = 48
BF16, F32, I32 = jnp.bfloat16, jnp.float32, jnp.int32
VMEM_BYTES = 24 * 2**20
LOW = -1e30


def dot(a, b):
    return jnp.dot(a, b, preferred_element_type=F32)


def nt(a, b):
    return lax.dot_general(a, b, (((1,), (1,)), ((), ())), preferred_element_type=F32)


def tn(a, b):
    return lax.dot_general(a, b, (((0,), (0,)), ((), ())), preferred_element_type=F32)


def cost(flops, moved, exps=0):
    return pl.CostEstimate(flops=int(flops), bytes_accessed=int(moved), transcendentals=int(exps))


def near_of(*dims, dtype=BF16):
    return pltpu.VMEM(dims, dtype)


def far_of(*dims, dtype=BF16):
    return pltpu.HBM(dims, dtype)


def near(a):
    return pltpu.with_memory_space_constraint(a, pltpu.VMEM)


def far(a):
    return pltpu.with_memory_space_constraint(a, pltpu.HBM)


def kernel_call(body, name, near_args, far_args, outs, scratch, price, aliases=None):
    in_vmem, anywhere = pl.BlockSpec(memory_space=pltpu.VMEM), pl.BlockSpec(memory_space=pl.ANY)
    return pl.pallas_call(
        body,
        in_specs=[in_vmem] * len(near_args) + [anywhere] * len(far_args),
        out_specs=[in_vmem if o.memory_space == pltpu.VMEM else anywhere for o in outs],
        out_shape=outs,
        scratch_shapes=scratch,
        input_output_aliases=aliases or {},
        compiler_params=pltpu.CompilerParams(vmem_limit_bytes=VMEM_BYTES),
        cost_estimate=price,
        name=name,
    )(*[near(a) for a in near_args], *[far(a) for a in far_args])


def head_spread(channels, pad):
    dim = channels // HEADS
    shape = (HEADS * pad, channels)
    row = lax.broadcasted_iota(I32, shape, 0)
    col = lax.broadcasted_iota(I32, shape, 1)
    head = sum((row >= h * pad).astype(I32) for h in range(1, HEADS))
    inside = row - head * pad
    return jnp.where((inside < dim) & (head * dim + inside == col), 1.0, 0.0).astype(BF16)


def project_kernel(x_hbm, g_hbm, wq_hbm, wk_hbm, wv_hbm, wo_hbm,
                   qt_ref, main_ref, first_ref, last_ref, wkp_ref, wvt_ref, wop_ref,
                   x_ref, g_ref, w_ref, x_sem, w_sem):
    frames, tok, ch = x_ref.shape
    copies = [pltpu.make_async_copy(g_hbm, g_ref, w_sem.at[4])]
    copies += [pltpu.make_async_copy(x_hbm.at[f], x_ref.at[f], x_sem.at[f]) for f in range(frames)]
    weights = [pltpu.make_async_copy(w, w_ref.at[k], w_sem.at[k])
               for k, w in enumerate((wq_hbm, wk_hbm, wv_hbm, wo_hbm))]
    for copy in copies + weights:
        copy.start()
    ek, ev = head_spread(ch, KPAD), head_spread(ch, VPAD)
    copies[0].wait()
    gain = jnp.broadcast_to(g_ref[...].astype(F32).reshape(1, ch), (8, ch)).T[:, 0:1]

    def normed(f):
        copies[1 + f].wait()
        floated = x_ref[f].astype(F32).T
        centre = floated - jnp.sum(floated, axis=0, keepdims=True) / ch
        spread = jnp.sum(centre * centre, axis=0, keepdims=True) / ch
        return (centre * lax.rsqrt(spread + 1e-05) * gain).astype(BF16)

    for f in range(frames):
        value = normed(f)
        if f < frames - 1:
            main_ref[f] = value
        else:
            last_ref[0] = value
        if f == 0:
            first_ref[0] = value
            for copy in weights:
                copy.wait()
            wqt = nt(ek, w_ref[0]).astype(BF16)
            wkp_ref[...] = nt(w_ref[1], ek).astype(BF16)
            wvt_ref[...] = nt(ev, w_ref[2]).astype(BF16)
            wop_ref[...] = dot(ev, w_ref[3]).astype(BF16)
        qt_ref[f] = dot(wqt, value).astype(BF16)


def project(x, gain, wq, wk, wv, wo):
    frames, tok, ch = x.shape
    nk, nv = HEADS * KPAD, HEADS * VPAD
    outs = [near_of(frames, nk, tok), near_of(frames - 1, ch, tok), near_of(1, ch, tok), near_of(1, ch, tok),
            near_of(ch, nk), near_of(nv, ch), near_of(nv, ch)]
    scratch = [pltpu.VMEM(x.shape, BF16), pltpu.VMEM((ch,), BF16), pltpu.VMEM((4, ch, ch), BF16),
               pltpu.SemaphoreType.DMA((frames,)), pltpu.SemaphoreType.DMA((5,))]
    return kernel_call(project_kernel, "project", [], [x, gain, wq, wk, wv, wo], outs, scratch,
                       cost(frames * tok * ch * nk, 8e5))


class Flash:
    def __init__(self, qt_ref, wkp_ref, wvt_ref, state_in, state_out, scratch):
        self.qt, self.wkp, self.wvt = qt_ref, wkp_ref, wvt_ref
        self.state_in, self.state_out = state_in, state_out
        self.acc, self.s, self.in_sem, self.out_sem, *kept = scratch
        if kept:
            self.k, self.vt = kept
        self.tok = qt_ref.shape[2]
        self.dim = wkp_ref.shape[0] // HEADS
        self.factor = math.log2(math.e) / math.sqrt(self.dim)

    def in_copy(self, f):
        return pltpu.make_async_copy(self.state_in.at[f], self.acc.at[f], self.in_sem.at[f])

    def out_copy(self, f):
        return pltpu.make_async_copy(self.acc.at[f], self.state_out.at[f], self.out_sem.at[f])

    def make_keys(self, seg):
        self.k[0:seg.shape[1], :] = tn(seg, self.wkp[...]).astype(BF16)

    def make_values(self, seg):
        keys = seg.shape[1]
        ones_row = lax.broadcasted_iota(I32, (16, keys), 0) == self.dim % 16
        vt = dot(self.wvt[...], seg).astype(BF16)
        for h in range(HEADS):
            at, end = h * VPAD + self.dim // 16 * 16, (h + 1) * VPAD
            self.vt[h * VPAD:at, 0:keys] = vt[h * VPAD:at]
            self.vt[at:at + 16, 0:keys] = jnp.where(ones_row, jnp.ones((16, keys), BF16), vt[at:at + 16])
            if at + 16 < end:
                self.vt[at + 16:end, 0:keys] = vt[at + 16:end]

    def scores(self, f, h, keys):
        own = self.qt[f, h * KPAD:(h + 1) * KPAD, :]
        zeros = jnp.zeros((KPAD, self.tok), BF16)
        both = jnp.concatenate([own, zeros] if h % 2 == 0 else [zeros, own], axis=0)
        lanes = h // 2 * 2 * KPAD
        self.s[h % 2, 0:keys] = dot(self.k[0:keys, lanes:lanes + 2 * KPAD], both)

    def begin(self, f, seg):
        self.make_keys(seg)
        self.make_values(seg)
        self.scores(f, 0, seg.shape[1])

    def item(self, f, keys, after=None, seg=None, first=False, attended=None):
        for h in range(HEADS):
            top = jnp.max(self.s[h % 2, 0:keys], axis=0, keepdims=True)
            if h + 1 < HEADS:
                self.scores(f, h + 1, keys)
            elif after is not None:
                if seg is not None:
                    self.make_keys(seg)
                self.scores(after, 0, keys if seg is None else seg.shape[1])
            rows = slice(h * VPAD, (h + 1) * VPAD)
            if not first:
                kept = self.acc[f, rows, :]
                old = kept[self.dim + 1:self.dim + 2]
                top = jnp.maximum(top, old)
            weights = jnp.exp2((self.s[h % 2, 0:keys] - top) * self.factor).astype(BF16)
            part = dot(self.vt[rows, 0:keys], weights)
            if not first:
                part = part + kept * jnp.exp2((old - top) * self.factor)
            if attended is not None:
                attended[rows, :] = (part / part[self.dim:self.dim + 1]).astype(BF16)
            else:
                self.acc[f, rows, :] = part
                self.acc[f, h * VPAD + self.dim + 1:h * VPAD + self.dim + 2, :] = top
        if after is not None and seg is not None:
            self.make_values(seg)


def own_kernel(qt_ref, wkp_ref, wvt_ref, main_ref, state_out, *scratch):
    flash = Flash(qt_ref, wkp_ref, wvt_ref, None, state_out, scratch)
    frames, keys = qt_ref.shape[0], main_ref.shape[2]
    flash.begin(1, main_ref[0])

    @pl.loop(1, frames - 1)
    def _(f):
        flash.item(f, keys, f + 1, main_ref[f], first=True)
        flash.out_copy(f).start()

    flash.item(frames - 1, keys, first=True)
    flash.out_copy(frames - 1).start()
    for f in range(1, frames):
        flash.out_copy(f).wait()


def side_kernel(qt_ref, wkp_ref, wvt_ref, prev_ref, main_ref, side_ref, state_in, state_out, *scratch):
    flash = Flash(qt_ref, wkp_ref, wvt_ref, state_in, state_out, scratch)
    frames, keys = qt_ref.shape[0], side_ref.shape[2]
    for f in range(1, frames):
        flash.in_copy(f).start()
    flash.begin(0, jnp.where(lax.axis_index("frame") > 0, prev_ref[0], main_ref[0]))
    flash.item(0, prev_ref.shape[2], 1, side_ref[0], first=True)
    flash.out_copy(0).start()

    @pl.loop(1, frames - 1)
    def _(f):
        flash.in_copy(f).wait()
        flash.item(f, keys, f + 1, side_ref[f])
        flash.out_copy(f).start()

    flash.in_copy(frames - 1).wait()
    flash.item(frames - 1, keys)
    flash.out_copy(frames - 1).start()
    for f in range(frames):
        flash.out_copy(f).wait()


def lead_kernel(qt_ref, wkp_ref, wvt_ref, prev_ref, side_ref, lead_ref, state_in, state_out, *scratch):
    flash = Flash(qt_ref, wkp_ref, wvt_ref, state_in, state_out, scratch)
    frames, keys = qt_ref.shape[0], lead_ref.shape[2]
    for f in range(frames):
        flash.in_copy(f).start()
    flash.begin(0, jnp.where(lax.axis_index("frame") > 0, prev_ref[0], side_ref[0]))
    flash.in_copy(0).wait()
    flash.item(0, prev_ref.shape[2], 0, lead_ref[0])
    flash.item(0, keys, 1)
    flash.out_copy(0).start()

    @pl.loop(1, frames - 1)
    def _(f):
        flash.in_copy(f).wait()
        flash.item(f, keys, f + 1)
        flash.out_copy(f).start()

    flash.in_copy(frames - 1).wait()
    flash.item(frames - 1, keys)
    flash.out_copy(frames - 1).start()
    for f in range(frames):
        flash.out_copy(f).wait()


def finish_kernel(start, rows, pair, fresh, *refs):
    refs = list(refs)
    take = lambda n: [refs.pop(0) for _ in range(n)]
    qt_ref, wkp_ref, wvt_ref, wop_ref = take(4)
    if fresh:
        (seg_ref,) = take(1)
    else:
        k_ref, vt_ref = take(2)
    state_hbm, x_hbm, upd_ref, edge_ref, stat_ref = take(5)
    if fresh:
        k_ref, vt_ref = take(2)
    att_ref, x_ref, x_sem = take(3)
    count, tok, ch = x_ref.shape
    cols, keys = tok // rows, k_ref.shape[0]
    flash = Flash(qt_ref, wkp_ref, wvt_ref, state_hbm, None, refs)
    flash.k, flash.vt = k_ref, vt_ref
    for f in range(start, start + count):
        flash.in_copy(f).start()
    copy = pltpu.make_async_copy(x_hbm.at[pl.ds(start, count)], x_ref, x_sem)
    copy.start()
    if fresh:
        flash.begin(start, seg_ref[0])
    else:
        flash.scores(start, 0, keys)

    @pl.loop(0, count)
    def _(i):
        flash.in_copy(start + i).wait()
        flash.item(start + i, keys, start + jnp.minimum(i + 1, count - 1), attended=att_ref)

        @pl.when(i == 0)
        def _():
            copy.wait()

        mixed = tn(att_ref[...], wop_ref[...])
        updated = (x_ref[i].astype(F32) + mixed).astype(BF16)
        upd_ref[i] = updated
        floated = updated.astype(F32)
        sums = jnp.sum(floated, axis=0, keepdims=True)
        squares = jnp.sum(floated * floated, axis=0, keepdims=True)
        which = lax.broadcasted_iota(I32, (8, ch), 0)
        stats = jnp.where(which == 0, sums, jnp.where(which == 1, squares, 0.0))
        stat_ref[i] = stats
        if pair:
            edge_ref[i, 0:cols] = jnp.where(lax.axis_index("row") == 0, floated[tok - cols:], floated[:cols])
            edge_ref[i, cols:cols + 8] = stats
        else:
            edge_ref[i, 0:cols] = floated[:cols]
            edge_ref[i, cols:2 * cols] = floated[tok - cols:]


def flash_scratch(qt, keys, held=True):
    frames, nk, tok = qt.shape
    nv = HEADS * VPAD
    out = [pltpu.VMEM((frames, nv, tok), F32), pltpu.VMEM((2, keys, tok), F32)]
    out += [pltpu.SemaphoreType.DMA((frames,))] * 2
    return out + ([pltpu.VMEM((keys, nk), BF16), pltpu.VMEM((nv, keys), BF16)] if held else [])


def flash_cost(items, keys, tok):
    made = items * HEADS * keys * tok
    return cost(made * 140, made // 80, made // 10)


def flash(body, name, qt, wkp, wvt, segments, state, items):
    frames, _, tok = qt.shape
    keys = max(s.shape[2] for s in segments)
    near_args, far_args = [qt, wkp, wvt] + segments, []
    aliases = {}
    if state is not None:
        far_args.append(state)
        aliases = {len(near_args): 0}
    outs = [far_of(frames, HEADS * VPAD, tok, dtype=F32)]
    return kernel_call(body, name, near_args, far_args, outs, flash_scratch(qt, keys),
                       flash_cost(items, keys, tok), aliases)[0]


def finish(start, count, qt, wkp, wvt, wop, state, lead_side, made, x, rows, pair):
    tok, ch = x.shape[1:]
    cols, nk, nv, keys = tok // rows, HEADS * KPAD, HEADS * VPAD, lead_side.shape[2]
    fresh = made is None
    outs = [near_of(count, tok, ch), near_of(count, cols + 8 if pair else 2 * cols, ch, dtype=F32),
            near_of(count, 8, ch, dtype=F32)]
    if fresh:
        outs += [near_of(keys, nk), near_of(nv, keys)]
    scratch = [pltpu.VMEM((nv, tok), BF16), pltpu.VMEM((count, tok, ch), BF16), pltpu.SemaphoreType.DMA]
    got = kernel_call(functools.partial(finish_kernel, start, rows, pair, fresh), "finish",
                      [qt, wkp, wvt, wop] + ([lead_side] if fresh else list(made)), [state, x], outs,
                      scratch + flash_scratch(qt, keys, held=False), flash_cost(count, keys, tok))
    return got[:3], (tuple(got[3:]) if fresh else made)


def conv_kernel(start, rows, counted, pair, fresh, *refs):
    refs = list(refs)
    take = lambda n: [refs.pop(0) for _ in range(n)]
    upd_ref, top_ref, bot_ref, stat_ref, gn_ref, bias_ref, w_ref = take(7)
    if not fresh:
        take(1)
    (out_hbm,) = take(1)
    if fresh:
        (wide_ref,) = take(1)
    act_ref, out_ref, sems = refs
    count, tok, ch = upd_ref.shape
    cols = tok // rows
    if fresh:
        for a in range(3):
            for b in range(3):
                wide_ref[a * ch:(a + 1) * ch, b * ch:(b + 1) * ch] = w_ref[a, b]
    else:
        wide_ref = w_ref

    stats = jnp.concatenate([stat_ref[i] + top_ref[i, cols:cols + 8] if pair else stat_ref[i]
                             for i in range(count)], axis=0)
    width = ch // GROUPS
    first = lax.broadcasted_iota(I32, (ch, ch), 0)
    second = lax.broadcasted_iota(I32, (ch, ch), 1)
    group_of = lambda v: (v * (65536 // width + 1)) >> 16
    same = jnp.where(group_of(first) == group_of(second), 1.0, 0.0).astype(BF16)
    high = stats.astype(BF16)
    rest = stats - high.astype(F32)
    middle = rest.astype(BF16)
    low = (rest - middle.astype(F32)).astype(BF16)
    grouped = (dot(high, same) + dot(middle, same) + dot(low, same)) / counted
    gain = gn_ref[...].astype(F32).reshape(1, ch)
    bias = bias_ref[...].astype(F32).reshape(1, ch)
    me = lax.axis_index("row")
    column = lax.broadcasted_iota(I32, (tok, ch), 0) % cols
    copies = []
    for i in range(count):
        mean = grouped[8 * i:8 * i + 1]
        scale = lax.rsqrt(grouped[8 * i + 1:8 * i + 2] - mean * mean + 1e-05) * gain

        def activated(u):
            v = (u.astype(F32) - mean) * scale
            return (v / (1.0 + jnp.exp(-v))).astype(BF16)

        above = jnp.where(me > 0, activated(top_ref[i, 0:cols]), jnp.zeros((cols, ch), BF16))
        below = jnp.where(me < lax.axis_size("row") - 1, activated(bot_ref[i, 0:cols]), jnp.zeros((cols, ch), BF16))
        inner = activated(upd_ref[i])
        act_ref[:, ch:2 * ch] = inner
        act_ref[0:cols, 0:ch] = above
        act_ref[cols:tok, 0:ch] = inner[0:tok - cols]
        act_ref[0:tok - cols, 2 * ch:] = inner[cols:tok]
        act_ref[tok - cols:tok, 2 * ch:] = below
        parts = dot(act_ref[...], wide_ref[...])
        left = jnp.where(column == 0, 0.0, pltpu.roll(parts[:, 0:ch], 1, 0))
        right = jnp.where(column == cols - 1, 0.0, pltpu.roll(parts[:, 2 * ch:], tok - 1, 0))
        out_ref[i] = (upd_ref[i].astype(F32) + (left + parts[:, ch:2 * ch] + right) + bias).astype(BF16)
        copies.append(pltpu.make_async_copy(out_ref.at[i], out_hbm.at[start + i], sems.at[i]))
        copies[-1].start()
    for copy in copies:
        copy.wait()


def conv(start, frames, upd, top, bot, stats, gn, bias, weight, rows, pair, counted, into=None):
    count, tok, ch = upd.shape
    fresh = into is None
    args = [upd, top, bot, stats, gn, bias, weight if fresh else into[1]]
    outs = [far_of(frames, tok, ch)] + ([near_of(3 * ch, 3 * ch)] if fresh else [])
    scratch = [pltpu.VMEM((tok, 3 * ch), BF16), pltpu.VMEM((count, tok, ch), BF16),
               pltpu.SemaphoreType.DMA((count,))]
    got = kernel_call(functools.partial(conv_kernel, start, rows, counted, pair, fresh), "conv",
                      args, [] if fresh else [into[0]], outs, scratch, cost(count * tok * ch * ch * 30, 4e6),
                      {} if fresh else {len(args): 0})
    return got[0], got[1] if fresh else into[1]


def fan(value, axis, heads, steps):
    size = lax.axis_size(axis)
    got = {}
    for k in steps:
        route = [(i, i + k) for i in heads if i + k < size]
        if route:
            got[k] = lax.ppermute(value, axis, route)
    return got


def chosen(value, axis, got, modulus):
    place = lax.axis_index(axis) % modulus
    for k, arrived in got.items():
        value = jnp.where(place == k, arrived, value)
    return value


def others(value, rows):
    got = [lax.ppermute(value, "row", [(i, (i + k) % rows) for i in range(rows)]) for k in range(1, rows)]
    return got[0] if len(got) == 1 else jnp.concatenate(got, axis=2)


def body(latents, ln_gain, q_weight, k_weight, v_weight, o_weight, gn_gain, conv_weight, conv_bias):
    frames, row_count, cols, ch = latents.shape
    tok = row_count * cols
    size, blocks = lax.axis_size("row"), lax.axis_size("frame")
    pair = size == 2
    x = latents.reshape(frames, tok, ch)

    qt, main, lead, tail, wkp, wvt, wop = project(x, ln_gain, q_weight, k_weight, v_weight, o_weight)
    common = (qt, wkp, wvt)
    routes = [[(f * size + r, (f + 1) * size + (r + k) % size) for f in range(blocks - 1) for r in range(size)]
              for k in range(size)]
    inner = 1
    while inner * inner < blocks:
        inner *= 2
    side = others(main, size)
    prev = lax.ppermute(tail, ("frame", "row"), routes[0])
    spread = fan(lead, "frame", [0], range(inner, blocks, inner))
    state = flash(own_kernel, "own", *common, [main], None, frames - 1)

    state, spread = lax.optimization_barrier((state, spread))
    side, tail = lax.optimization_barrier((side, tail))
    came = [lax.ppermute(tail, ("frame", "row"), route) for route in routes[1:]]
    prev_side = came[0] if pair else jnp.concatenate(came, axis=2)
    lead = chosen(lead, "frame", spread, blocks)
    spread = fan(lead, "frame", range(0, blocks, inner), range(1, inner))
    state = flash(side_kernel, "side", *common, [prev, main, side], state, frames)

    state, spread = lax.optimization_barrier((state, spread))
    lead = chosen(lead, "frame", spread, inner)
    lead_side = others(lead, size)
    state = flash(lead_kernel, "lead", *common, [prev_side, side, lead], state, frames + 1)

    half = frames // 2
    made, into, finished = None, None, []
    for start, count in ((0, half), (half, frames - half)):
        (upd, edge, stats), made = finish(start, count, *common, wop, state, lead_side, made, x, row_count, pair)
        if pair:
            top = bot = lax.ppermute(edge, "row", [(0, 1), (1, 0)])
        else:
            top = lax.ppermute(edge[:, cols:], "row", [(i, i + 1) for i in range(size - 1)])
            bot = lax.ppermute(edge[:, :cols], "row", [(i + 1, i) for i in range(size - 1)])
            stats = lax.psum(stats, "row")
        finished.append((start, upd, top, bot, stats))
    for start, upd, top, bot, stats in finished:
        into = conv(start, frames, upd, top, bot, stats, gn_gain, conv_bias, conv_weight,
                    row_count, pair, tok * size * (ch // GROUPS), into)
    return into[0].reshape(latents.shape)


def solution(mesh):
    in_specs = (P("frame", "row", None, None), P(), P(), P(), P(), P(), P(), P(), P())
    out_specs = P("frame", "row", None, None)
    return jax.shard_map(body, mesh=mesh, in_specs=in_specs, out_specs=out_specs, check_vma=False)
```

```python
import functools
import math

import jax
import jax.numpy as jnp
from jax import lax
from jax.experimental import pallas as pl
from jax.experimental.pallas import tpu as pltpu
from jax.sharding import PartitionSpec as P

HEADS = 8
GROUPS = 32
KPAD = 64
VPAD = 48
BF16, F32, I32 = jnp.bfloat16, jnp.float32, jnp.int32
VMEM_BYTES = 24 * 2**20
LOW = -1e30


def dot(a, b):
    return jnp.dot(a, b, preferred_element_type=F32)


def nt(a, b):
    return lax.dot_general(a, b, (((1,), (1,)), ((), ())), preferred_element_type=F32)


def tn(a, b):
    return lax.dot_general(a, b, (((0,), (0,)), ((), ())), preferred_element_type=F32)


def cost(flops, moved, exps=0):
    return pl.CostEstimate(flops=int(flops), bytes_accessed=int(moved), transcendentals=int(exps))


def near_of(*dims, dtype=BF16):
    return pltpu.VMEM(dims, dtype)


def far_of(*dims, dtype=BF16):
    return pltpu.HBM(dims, dtype)


def near(a):
    return pltpu.with_memory_space_constraint(a, pltpu.VMEM)


def far(a):
    return pltpu.with_memory_space_constraint(a, pltpu.HBM)


def kernel_call(body, name, near_args, far_args, outs, scratch, price, aliases=None):
    in_vmem, anywhere = pl.BlockSpec(memory_space=pltpu.VMEM), pl.BlockSpec(memory_space=pl.ANY)
    return pl.pallas_call(
        body,
        in_specs=[in_vmem] * len(near_args) + [anywhere] * len(far_args),
        out_specs=[in_vmem if o.memory_space == pltpu.VMEM else anywhere for o in outs],
        out_shape=outs,
        scratch_shapes=scratch,
        input_output_aliases=aliases or {},
        compiler_params=pltpu.CompilerParams(vmem_limit_bytes=VMEM_BYTES),
        cost_estimate=price,
        name=name,
    )(*[near(a) for a in near_args], *[far(a) for a in far_args])


def head_spread(channels, pad):
    dim = channels // HEADS
    shape = (HEADS * pad, channels)
    row = lax.broadcasted_iota(I32, shape, 0)
    col = lax.broadcasted_iota(I32, shape, 1)
    head = sum((row >= h * pad).astype(I32) for h in range(1, HEADS))
    inside = row - head * pad
    return jnp.where((inside < dim) & (head * dim + inside == col), 1.0, 0.0).astype(BF16)


def project_kernel(x_hbm, g_hbm, wq_hbm, wk_hbm, wv_hbm, wo_hbm,
                   qt_ref, main_hbm, first_ref, last_ref, wkp_ref, wvt_ref, wop_ref,
                   x_ref, g_ref, w_ref, main_ref, x_sem, w_sem, main_sem):
    frames, tok, ch = x_ref.shape
    copies = [pltpu.make_async_copy(g_hbm, g_ref, w_sem.at[4])]
    copies += [pltpu.make_async_copy(x_hbm.at[f], x_ref.at[f], x_sem.at[f]) for f in range(frames)]
    weights = [pltpu.make_async_copy(w, w_ref.at[k], w_sem.at[k])
               for k, w in enumerate((wq_hbm, wk_hbm, wv_hbm, wo_hbm))]
    for copy in copies + weights:
        copy.start()
    ek, ev = head_spread(ch, KPAD), head_spread(ch, VPAD)
    copies[0].wait()
    gain = jnp.broadcast_to(g_ref[...].astype(F32).reshape(1, ch), (8, ch)).T[:, 0:1]

    def normed(f):
        copies[1 + f].wait()
        floated = x_ref[f].astype(F32).T
        centre = floated - jnp.sum(floated, axis=0, keepdims=True) / ch
        spread = jnp.sum(centre * centre, axis=0, keepdims=True) / ch
        return (centre * lax.rsqrt(spread + 1e-05) * gain).astype(BF16)

    leave = []
    for f in range(frames):
        value = normed(f)
        if f < frames - 1:
            main_ref[f] = value
            leave.append(pltpu.make_async_copy(main_ref.at[f], main_hbm.at[f], main_sem.at[f]))
            leave[-1].start()
        else:
            last_ref[0] = value
        if f == 0:
            first_ref[0] = value
            for copy in weights:
                copy.wait()
            wqt = nt(ek, w_ref[0]).astype(BF16)
            wkp_ref[...] = nt(w_ref[1], ek).astype(BF16)
            wvt_ref[...] = nt(ev, w_ref[2]).astype(BF16)
            wop_ref[...] = dot(ev, w_ref[3]).astype(BF16)
        qt_ref[f] = dot(wqt, value).astype(BF16)
    for copy in leave:
        copy.wait()


def project(x, gain, wq, wk, wv, wo):
    frames, tok, ch = x.shape
    nk, nv = HEADS * KPAD, HEADS * VPAD
    outs = [near_of(frames, nk, tok), far_of(frames - 1, ch, tok), near_of(1, ch, tok), near_of(1, ch, tok),
            near_of(ch, nk), near_of(nv, ch), near_of(nv, ch)]
    scratch = [pltpu.VMEM(x.shape, BF16), pltpu.VMEM((ch,), BF16), pltpu.VMEM((4, ch, ch), BF16),
               pltpu.VMEM((frames - 1, ch, tok), BF16), pltpu.SemaphoreType.DMA((frames,)),
               pltpu.SemaphoreType.DMA((5,)), pltpu.SemaphoreType.DMA((frames - 1,))]
    return kernel_call(project_kernel, "project", [], [x, gain, wq, wk, wv, wo], outs, scratch,
                       cost(frames * tok * ch * nk, 8e5))


class Flash:
    def __init__(self, qt_ref, wkp_ref, wvt_ref, state_in, state_out, scratch):
        self.qt, self.wkp, self.wvt = qt_ref, wkp_ref, wvt_ref
        self.state_in, self.state_out = state_in, state_out
        self.acc, self.s, self.in_sem, self.out_sem, *kept = scratch
        if kept:
            self.k, self.vt = kept
        self.tok = qt_ref.shape[2]
        self.dim = wkp_ref.shape[0] // HEADS
        self.factor = math.log2(math.e) / math.sqrt(self.dim)

    def in_copy(self, f):
        return pltpu.make_async_copy(self.state_in.at[f], self.acc.at[f], self.in_sem.at[f])

    def out_copy(self, f):
        return pltpu.make_async_copy(self.acc.at[f], self.state_out.at[f], self.out_sem.at[f])

    def part_copy(self, f, h):
        rows = pl.ds((h - 1) * VPAD, 2 * VPAD)
        return pltpu.make_async_copy(self.acc.at[f, rows], self.state_out.at[f, rows], self.out_sem.at[f])

    def make_keys(self, seg):
        self.k[0:seg.shape[1], :] = tn(seg, self.wkp[...]).astype(BF16)

    def make_values(self, seg):
        keys = seg.shape[1]
        ones_row = lax.broadcasted_iota(I32, (16, keys), 0) == self.dim % 16
        vt = dot(self.wvt[...], seg).astype(BF16)
        for h in range(HEADS):
            at, end = h * VPAD + self.dim // 16 * 16, (h + 1) * VPAD
            self.vt[h * VPAD:at, 0:keys] = vt[h * VPAD:at]
            self.vt[at:at + 16, 0:keys] = jnp.where(ones_row, jnp.ones((16, keys), BF16), vt[at:at + 16])
            if at + 16 < end:
                self.vt[at + 16:end, 0:keys] = vt[at + 16:end]

    def scores(self, f, h, keys):
        own = self.qt[f, h * KPAD:(h + 1) * KPAD, :]
        zeros = jnp.zeros((KPAD, self.tok), BF16)
        both = jnp.concatenate([own, zeros] if h % 2 == 0 else [zeros, own], axis=0)
        lanes = h // 2 * 2 * KPAD
        self.s[h % 2, 0:keys] = dot(self.k[0:keys, lanes:lanes + 2 * KPAD], both)

    def begin(self, f, seg):
        self.make_keys(seg)
        self.make_values(seg)
        self.scores(f, 0, seg.shape[1])

    def item(self, f, keys, after=None, seg=None, first=False, attended=None, leave=False):
        for h in range(HEADS):
            top = jnp.max(self.s[h % 2, 0:keys], axis=0, keepdims=True)
            if h + 1 < HEADS:
                self.scores(f, h + 1, keys)
            elif after is not None:
                if seg is not None:
                    self.make_keys(seg)
                self.scores(after, 0, keys if seg is None else seg.shape[1])
            rows = slice(h * VPAD, (h + 1) * VPAD)
            if not first:
                kept = self.acc[f, rows, :]
                old = kept[self.dim + 1:self.dim + 2]
                top = jnp.maximum(top, old)
            weights = jnp.exp2((self.s[h % 2, 0:keys] - top) * self.factor).astype(BF16)
            part = dot(self.vt[rows, 0:keys], weights)
            if not first:
                part = part + kept * jnp.exp2((old - top) * self.factor)
            if attended is not None:
                attended[rows, :] = (part / part[self.dim:self.dim + 1]).astype(BF16)
            else:
                self.acc[f, rows, :] = part
                self.acc[f, h * VPAD + self.dim + 1:h * VPAD + self.dim + 2, :] = top
                if leave and h % 2 == 1:
                    self.part_copy(f, h).start()
        if after is not None and seg is not None:
            self.make_values(seg)


class Arriving:
    def __init__(self, hbm, near_ref, sem, start=0):
        self.hbm, self.near, self.sem = hbm, near_ref, sem
        for k in range(start, hbm.shape[0]):
            self.copy(k).start()

    def copy(self, k):
        return pltpu.make_async_copy(self.hbm.at[k], self.near.at[k], self.sem.at[k])

    def __getitem__(self, k):
        self.copy(k).wait()
        return self.near[k]


def own_kernel(qt_ref, wkp_ref, wvt_ref, first_ref, main_hbm, state_out, main_near, main_sem, *scratch):
    flash = Flash(qt_ref, wkp_ref, wvt_ref, None, state_out, scratch)
    frames, keys = qt_ref.shape[0], main_hbm.shape[2]
    main = Arriving(main_hbm, main_near, main_sem, 1)
    flash.begin(1, first_ref[0])

    @pl.loop(1, frames - 1)
    def _(f):
        flash.item(f, keys, f + 1, main[f], first=True)
        flash.out_copy(f).start()

    flash.item(frames - 1, keys, first=True, leave=True)
    for f in range(1, frames):
        flash.out_copy(f).wait()


def side_kernel(qt_ref, wkp_ref, wvt_ref, prev_ref, first_ref, side_hbm, state_in, state_out, mirror_ref,
                side_near, side_sem, *scratch):
    flash = Flash(qt_ref, wkp_ref, wvt_ref, state_in, state_out, scratch)
    frames, keys = qt_ref.shape[0], side_hbm.shape[2]
    side = Arriving(side_hbm, side_near, side_sem)
    for f in range(1, frames):
        flash.in_copy(f).start()
    flash.begin(0, jnp.where(lax.axis_index("frame") > 0, prev_ref[0], first_ref[0]))
    leading = side[0]
    mirror_ref[0] = leading
    flash.item(0, prev_ref.shape[2], 1, leading, first=True)
    flash.out_copy(0).start()

    @pl.loop(1, frames - 1)
    def _(f):
        flash.in_copy(f).wait()
        flash.item(f, keys, f + 1, side[f])
        flash.out_copy(f).start()

    flash.in_copy(frames - 1).wait()
    flash.item(frames - 1, keys, leave=True)
    for f in range(frames):
        flash.out_copy(f).wait()


def lead_kernel(qt_ref, wkp_ref, wvt_ref, prev_ref, mirror_ref, lead_ref, state_in, state_out, *scratch):
    flash = Flash(qt_ref, wkp_ref, wvt_ref, state_in, state_out, scratch)
    frames, keys = qt_ref.shape[0], lead_ref.shape[2]
    for f in range(frames):
        flash.in_copy(f).start()
    flash.begin(0, jnp.where(lax.axis_index("frame") > 0, prev_ref[0], mirror_ref[0]))
    flash.in_copy(0).wait()
    flash.item(0, prev_ref.shape[2], 0, lead_ref[0])
    flash.item(0, keys, 1)
    flash.out_copy(0).start()

    @pl.loop(1, frames - 1)
    def _(f):
        flash.in_copy(f).wait()
        flash.item(f, keys, f + 1)
        flash.out_copy(f).start()

    flash.in_copy(frames - 1).wait()
    flash.item(frames - 1, keys, leave=True)
    for f in range(frames):
        flash.out_copy(f).wait()


def finish_kernel(start, rows, pair, fresh, *refs):
    refs = list(refs)
    take = lambda n: [refs.pop(0) for _ in range(n)]
    qt_ref, wkp_ref, wvt_ref, wop_ref = take(4)
    if fresh:
        (seg_ref,) = take(1)
    else:
        k_ref, vt_ref = take(2)
    state_hbm, x_hbm, upd_ref, edge_ref, stat_ref = take(5)
    if fresh:
        k_ref, vt_ref = take(2)
    att_ref, x_ref, x_sem = take(3)
    count, tok, ch = x_ref.shape
    cols, keys = tok // rows, k_ref.shape[0]
    flash = Flash(qt_ref, wkp_ref, wvt_ref, state_hbm, None, refs)
    flash.k, flash.vt = k_ref, vt_ref
    for f in range(start, start + count):
        flash.in_copy(f).start()
    copy = pltpu.make_async_copy(x_hbm.at[pl.ds(start, count)], x_ref, x_sem)
    copy.start()
    if fresh:
        flash.begin(start, seg_ref[0])
    else:
        flash.scores(start, 0, keys)

    @pl.loop(0, count)
    def _(i):
        flash.in_copy(start + i).wait()
        flash.item(start + i, keys, start + jnp.minimum(i + 1, count - 1), attended=att_ref)

        @pl.when(i == 0)
        def _():
            copy.wait()

        mixed = tn(att_ref[...], wop_ref[...])
        updated = (x_ref[i].astype(F32) + mixed).astype(BF16)
        upd_ref[i] = updated
        floated = updated.astype(F32)
        sums = jnp.sum(floated, axis=0, keepdims=True)
        squares = jnp.sum(floated * floated, axis=0, keepdims=True)
        which = lax.broadcasted_iota(I32, (8, ch), 0)
        stats = jnp.where(which == 0, sums, jnp.where(which == 1, squares, 0.0))
        stat_ref[i] = stats
        if pair:
            edge_ref[i, 0:cols] = jnp.where(lax.axis_index("row") == 0, floated[tok - cols:], floated[:cols])
            edge_ref[i, cols:cols + 8] = stats
        else:
            edge_ref[i, 0:cols] = floated[:cols]
            edge_ref[i, cols:2 * cols] = floated[tok - cols:]


def flash_scratch(qt, keys, held=True):
    frames, nk, tok = qt.shape
    nv = HEADS * VPAD
    out = [pltpu.VMEM((frames, nv, tok), F32), pltpu.VMEM((2, keys, tok), F32)]
    out += [pltpu.SemaphoreType.DMA((frames,))] * 2
    return out + ([pltpu.VMEM((keys, nk), BF16), pltpu.VMEM((nv, keys), BF16)] if held else [])


def flash_cost(items, keys, tok):
    made = items * HEADS * keys * tok
    return cost(made * 140, made // 80, made // 10)


def flash(body, name, qt, wkp, wvt, segments, state, items, moved=None, mirrored=False):
    frames, _, tok = qt.shape
    keys = max(s.shape[2] for s in segments + ([] if moved is None else [moved]))
    near_args, far_args, scratch = [qt, wkp, wvt] + segments, [], []
    if moved is not None:
        far_args.append(moved)
        scratch = [pltpu.VMEM(moved.shape, BF16), pltpu.SemaphoreType.DMA((moved.shape[0],))]
    aliases = {}
    if state is not None:
        far_args.append(state)
        aliases = {len(near_args) + len(far_args) - 1: 0}
    outs = [far_of(frames, HEADS * VPAD, tok, dtype=F32)] + ([near_of(1, *moved.shape[1:])] if mirrored else [])
    got = kernel_call(body, name, near_args, far_args, outs, scratch + flash_scratch(qt, keys),
                      flash_cost(items, keys, tok), aliases)
    return got if mirrored else got[0]


def finish(start, count, qt, wkp, wvt, wop, state, lead_side, made, x, rows, pair):
    tok, ch = x.shape[1:]
    cols, nk, nv, keys = tok // rows, HEADS * KPAD, HEADS * VPAD, lead_side.shape[2]
    fresh = made is None
    outs = [near_of(count, tok, ch), near_of(count, cols + 8 if pair else 2 * cols, ch, dtype=F32),
            near_of(count, 8, ch, dtype=F32)]
    if fresh:
        outs += [near_of(keys, nk), near_of(nv, keys)]
    scratch = [pltpu.VMEM((nv, tok), BF16), pltpu.VMEM((count, tok, ch), BF16), pltpu.SemaphoreType.DMA]
    got = kernel_call(functools.partial(finish_kernel, start, rows, pair, fresh), "finish",
                      [qt, wkp, wvt, wop] + ([lead_side] if fresh else list(made)), [state, x], outs,
                      scratch + flash_scratch(qt, keys, held=False), flash_cost(count, keys, tok))
    return got[:3], (tuple(got[3:]) if fresh else made)


def conv_kernel(start, rows, counted, pair, fresh, *refs):
    refs = list(refs)
    take = lambda n: [refs.pop(0) for _ in range(n)]
    upd_ref, top_ref, bot_ref, stat_ref, gn_ref, bias_ref, w_ref = take(7)
    if not fresh:
        take(1)
    (out_hbm,) = take(1)
    if fresh:
        (wide_ref,) = take(1)
    act_ref, out_ref, sems = refs
    count, tok, ch = upd_ref.shape
    cols = tok // rows
    if fresh:
        for a in range(3):
            for b in range(3):
                wide_ref[a * ch:(a + 1) * ch, b * ch:(b + 1) * ch] = w_ref[a, b]
    else:
        wide_ref = w_ref

    stats = jnp.concatenate([stat_ref[i] + top_ref[i, cols:cols + 8] if pair else stat_ref[i]
                             for i in range(count)], axis=0)
    width = ch // GROUPS
    first = lax.broadcasted_iota(I32, (ch, ch), 0)
    second = lax.broadcasted_iota(I32, (ch, ch), 1)
    group_of = lambda v: (v * (65536 // width + 1)) >> 16
    same = jnp.where(group_of(first) == group_of(second), 1.0, 0.0).astype(BF16)
    high = stats.astype(BF16)
    rest = stats - high.astype(F32)
    middle = rest.astype(BF16)
    low = (rest - middle.astype(F32)).astype(BF16)
    grouped = (dot(high, same) + dot(middle, same) + dot(low, same)) / counted
    gain = gn_ref[...].astype(F32).reshape(1, ch)
    bias = bias_ref[...].astype(F32).reshape(1, ch)
    me = lax.axis_index("row")
    column = lax.broadcasted_iota(I32, (tok, ch), 0) % cols
    copies = []
    for i in range(count):
        mean = grouped[8 * i:8 * i + 1]
        scale = lax.rsqrt(grouped[8 * i + 1:8 * i + 2] - mean * mean + 1e-05) * gain

        def activated(u):
            v = (u.astype(F32) - mean) * scale
            half = 0.5 * v
            return (half + half * jnp.tanh(half)).astype(BF16)

        above = jnp.where(me > 0, activated(top_ref[i, 0:cols]), jnp.zeros((cols, ch), BF16))
        below = jnp.where(me < lax.axis_size("row") - 1, activated(bot_ref[i, 0:cols]), jnp.zeros((cols, ch), BF16))
        inner = activated(upd_ref[i])
        act_ref[:, ch:2 * ch] = inner
        act_ref[0:cols, 0:ch] = above
        act_ref[cols:tok, 0:ch] = inner[0:tok - cols]
        act_ref[0:tok - cols, 2 * ch:] = inner[cols:tok]
        act_ref[tok - cols:tok, 2 * ch:] = below
        parts = dot(act_ref[...], wide_ref[...])
        left = jnp.where(column == 0, 0.0, pltpu.roll(parts[:, 0:ch], 1, 0))
        right = jnp.where(column == cols - 1, 0.0, pltpu.roll(parts[:, 2 * ch:], tok - 1, 0))
        out_ref[i] = (upd_ref[i].astype(F32) + (left + parts[:, ch:2 * ch] + right) + bias).astype(BF16)
        copies.append(pltpu.make_async_copy(out_ref.at[i], out_hbm.at[start + i], sems.at[i]))
        copies[-1].start()
    for copy in copies:
        copy.wait()


def conv(start, frames, upd, top, bot, stats, gn, bias, weight, rows, pair, counted, into=None):
    count, tok, ch = upd.shape
    fresh = into is None
    args = [upd, top, bot, stats, gn, bias, weight if fresh else into[1]]
    outs = [far_of(frames, tok, ch)] + ([near_of(3 * ch, 3 * ch)] if fresh else [])
    scratch = [pltpu.VMEM((tok, 3 * ch), BF16), pltpu.VMEM((count, tok, ch), BF16),
               pltpu.SemaphoreType.DMA((count,))]
    got = kernel_call(functools.partial(conv_kernel, start, rows, counted, pair, fresh), "conv",
                      args, [] if fresh else [into[0]], outs, scratch, cost(count * tok * ch * ch * 30, 4e6),
                      {} if fresh else {len(args): 0})
    return got[0], got[1] if fresh else into[1]


def fan(value, axis, heads, steps):
    size = lax.axis_size(axis)
    got = {}
    for k in steps:
        route = [(i, i + k) for i in heads if i + k < size]
        if route:
            got[k] = lax.ppermute(value, axis, route)
    return got


def chosen_kernel(axis, modulus, places, *refs):
    place = lax.axis_index(axis) % modulus
    *sources, out_hbm, sem = refs
    elsewhere = place >= 0
    for k, source in zip(places, sources[1:]):
        here = place == k
        elsewhere = elsewhere & (place != k)

        @pl.when(here)
        def _(source=source):
            copy = pltpu.make_async_copy(source, out_hbm, sem)
            copy.start()
            copy.wait()

    @pl.when(elsewhere)
    def _():
        copy = pltpu.make_async_copy(sources[0], out_hbm, sem)
        copy.start()
        copy.wait()


def chosen(value, axis, got, modulus):
    anywhere = pl.BlockSpec(memory_space=pl.ANY)
    return pl.pallas_call(
        functools.partial(chosen_kernel, axis, modulus, tuple(got)),
        in_specs=[anywhere] * (1 + len(got)),
        out_specs=anywhere,
        out_shape=jax.ShapeDtypeStruct(value.shape, value.dtype),
        scratch_shapes=[pltpu.SemaphoreType.DMA],
        compiler_params=pltpu.CompilerParams(vmem_limit_bytes=VMEM_BYTES),
        cost_estimate=cost(0, 2 * value.size),
        name="chosen",
    )(value, *got.values())


def others(value, rows):
    got = [lax.ppermute(value, "row", [(i, (i + k) % rows) for i in range(rows)]) for k in range(1, rows)]
    return got[0] if len(got) == 1 else jnp.concatenate(got, axis=2)


def body(latents, ln_gain, q_weight, k_weight, v_weight, o_weight, gn_gain, conv_weight, conv_bias):
    frames, row_count, cols, ch = latents.shape
    tok = row_count * cols
    size, blocks = lax.axis_size("row"), lax.axis_size("frame")
    pair = size == 2
    x = latents.reshape(frames, tok, ch)

    qt, main, lead, tail, wkp, wvt, wop = project(x, ln_gain, q_weight, k_weight, v_weight, o_weight)
    common = (qt, wkp, wvt)
    routes = [[(f * size + r, (f + 1) * size + (r + k) % size) for f in range(blocks - 1) for r in range(size)]
              for k in range(size)]
    inner = 1
    while inner * inner < blocks:
        inner *= 2
    side = others(main, size)
    prev = lax.ppermute(tail, ("frame", "row"), routes[0])
    spread = fan(lead, "frame", [0], range(inner, blocks, inner))
    first = lead
    state = flash(own_kernel, "own", *common, [first], None, frames - 1, moved=main)

    state, spread = lax.optimization_barrier((state, spread))
    side, tail = lax.optimization_barrier((side, tail))
    came = [lax.ppermute(tail, ("frame", "row"), route) for route in routes[1:]]
    prev_side = came[0] if pair else jnp.concatenate(came, axis=2)
    lead = chosen(lead, "frame", spread, blocks)
    spread = fan(lead, "frame", range(0, blocks, inner), range(1, inner))
    state, mirror = flash(side_kernel, "side", *common, [prev, first], state, frames, moved=side, mirrored=True)

    state, spread = lax.optimization_barrier((state, spread))
    lead = chosen(lead, "frame", spread, inner)
    lead_side = others(lead, size)
    state = flash(lead_kernel, "lead", *common, [prev_side, mirror, lead], state, frames + 1)

    half = frames // 2
    made, into, finished = None, None, []
    for start, count in ((0, half), (half, frames - half)):
        (upd, edge, stats), made = finish(start, count, *common, wop, state, lead_side, made, x, row_count, pair)
        if pair:
            top = bot = lax.ppermute(edge, "row", [(0, 1), (1, 0)])
        else:
            top = lax.ppermute(edge[:, cols:], "row", [(i, i + 1) for i in range(size - 1)])
            bot = lax.ppermute(edge[:, :cols], "row", [(i + 1, i) for i in range(size - 1)])
            stats = lax.psum(stats, "row")
        finished.append((start, upd, top, bot, stats))
    for start, upd, top, bot, stats in finished:
        into = conv(start, frames, upd, top, bot, stats, gn_gain, conv_bias, conv_weight,
                    row_count, pair, tok * size * (ch // GROUPS), into)
    return into[0].reshape(latents.shape)


def solution(mesh):
    in_specs = (P("frame", "row", None, None), P(), P(), P(), P(), P(), P(), P(), P())
    out_specs = P("frame", "row", None, None)
    return jax.shard_map(body, mesh=mesh, in_specs=in_specs, out_specs=out_specs, check_vma=False)
```

```python
import functools
import math

import jax
import jax.numpy as jnp
from jax import lax
from jax.experimental import pallas as pl
from jax.experimental.pallas import tpu as pltpu
from jax.sharding import PartitionSpec as P

HEADS = 8
GROUPS = 32
KPAD = 64
VPAD = 48
BF16, F32, I32 = jnp.bfloat16, jnp.float32, jnp.int32
VMEM_BYTES = 24 * 2**20
LOW = -1e30


def dot(a, b):
    return jnp.dot(a, b, preferred_element_type=F32)


def nt(a, b):
    return lax.dot_general(a, b, (((1,), (1,)), ((), ())), preferred_element_type=F32)


def tn(a, b):
    return lax.dot_general(a, b, (((0,), (0,)), ((), ())), preferred_element_type=F32)


def cost(flops, moved, exps=0):
    return pl.CostEstimate(flops=int(flops), bytes_accessed=int(moved), transcendentals=int(exps))


def near_of(*dims, dtype=BF16):
    return pltpu.VMEM(dims, dtype)


def far_of(*dims, dtype=BF16):
    return pltpu.HBM(dims, dtype)


def near(a):
    return pltpu.with_memory_space_constraint(a, pltpu.VMEM)


def far(a):
    return pltpu.with_memory_space_constraint(a, pltpu.HBM)


def kernel_call(body, name, near_args, far_args, outs, scratch, price, aliases=None):
    in_vmem, anywhere = pl.BlockSpec(memory_space=pltpu.VMEM), pl.BlockSpec(memory_space=pl.ANY)
    return pl.pallas_call(
        body,
        in_specs=[in_vmem] * len(near_args) + [anywhere] * len(far_args),
        out_specs=[in_vmem if o.memory_space == pltpu.VMEM else anywhere for o in outs],
        out_shape=outs,
        scratch_shapes=scratch,
        input_output_aliases=aliases or {},
        compiler_params=pltpu.CompilerParams(vmem_limit_bytes=VMEM_BYTES),
        cost_estimate=price,
        name=name,
    )(*[near(a) for a in near_args], *[far(a) for a in far_args])


def head_spread(channels, pad):
    dim = channels // HEADS
    shape = (HEADS * pad, channels)
    row = lax.broadcasted_iota(I32, shape, 0)
    col = lax.broadcasted_iota(I32, shape, 1)
    head = sum((row >= h * pad).astype(I32) for h in range(1, HEADS))
    inside = row - head * pad
    return jnp.where((inside < dim) & (head * dim + inside == col), 1.0, 0.0).astype(BF16)


def project_kernel(x_hbm, g_hbm, wq_hbm, wk_hbm, wv_hbm, wo_hbm,
                   qt_ref, main_hbm, first_ref, last_ref, wkp_ref, wvt_ref, wop_ref,
                   x_ref, g_ref, w_ref, main_ref, x_sem, w_sem, main_sem):
    frames, tok, ch = x_ref.shape
    copies = [pltpu.make_async_copy(g_hbm, g_ref, w_sem.at[4])]
    copies += [pltpu.make_async_copy(x_hbm.at[f], x_ref.at[f], x_sem.at[f]) for f in range(frames)]
    weights = [pltpu.make_async_copy(w, w_ref.at[k], w_sem.at[k])
               for k, w in enumerate((wq_hbm, wk_hbm, wv_hbm, wo_hbm))]
    for copy in copies + weights:
        copy.start()
    ek, ev = head_spread(ch, KPAD), head_spread(ch, VPAD)
    copies[0].wait()
    gain = jnp.broadcast_to(g_ref[...].astype(F32).reshape(1, ch), (8, ch)).T[:, 0:1]

    def normed(f):
        copies[1 + f].wait()
        floated = x_ref[f].astype(F32).T
        centre = floated - jnp.sum(floated, axis=0, keepdims=True) / ch
        spread = jnp.sum(centre * centre, axis=0, keepdims=True) / ch
        return (centre * lax.rsqrt(spread + 1e-05) * gain).astype(BF16)

    leave = []
    for f in range(frames):
        value = normed(f)
        if f < frames - 1:
            main_ref[f] = value
            leave.append(pltpu.make_async_copy(main_ref.at[f], main_hbm.at[f], main_sem.at[f]))
            leave[-1].start()
        else:
            last_ref[0] = value
        if f == 0:
            first_ref[0] = value
            for copy in weights:
                copy.wait()
            wqt = nt(ek, w_ref[0]).astype(BF16)
            wkp_ref[...] = nt(w_ref[1], ek).astype(BF16)
            wvt_ref[...] = nt(ev, w_ref[2]).astype(BF16)
            wop_ref[...] = dot(ev, w_ref[3]).astype(BF16)
        qt_ref[f] = dot(wqt, value).astype(BF16)
    for copy in leave:
        copy.wait()


def project(x, gain, wq, wk, wv, wo):
    frames, tok, ch = x.shape
    nk, nv = HEADS * KPAD, HEADS * VPAD
    outs = [near_of(frames, nk, tok), far_of(frames - 1, ch, tok), near_of(1, ch, tok), near_of(1, ch, tok),
            near_of(ch, nk), near_of(nv, ch), near_of(nv, ch)]
    scratch = [pltpu.VMEM(x.shape, BF16), pltpu.VMEM((ch,), BF16), pltpu.VMEM((4, ch, ch), BF16),
               pltpu.VMEM((frames - 1, ch, tok), BF16), pltpu.SemaphoreType.DMA((frames,)),
               pltpu.SemaphoreType.DMA((5,)), pltpu.SemaphoreType.DMA((frames - 1,))]
    return kernel_call(project_kernel, "project", [], [x, gain, wq, wk, wv, wo], outs, scratch,
                       cost(frames * tok * ch * nk, 8e5))


class Flash:
    def __init__(self, qt_ref, wkp_ref, wvt_ref, state_in, state_out, scratch):
        self.qt, self.wkp, self.wvt = qt_ref, wkp_ref, wvt_ref
        self.state_in, self.state_out = state_in, state_out
        self.acc, self.s, self.in_sem, self.out_sem, *kept = scratch
        if kept:
            self.k, self.vt = kept
        self.tok = qt_ref.shape[2]
        self.dim = wkp_ref.shape[0] // HEADS
        self.factor = math.log2(math.e) / math.sqrt(self.dim)

    def in_copy(self, f):
        return pltpu.make_async_copy(self.state_in.at[f], self.acc.at[f], self.in_sem.at[f])

    def out_copy(self, f):
        return pltpu.make_async_copy(self.acc.at[f], self.state_out.at[f], self.out_sem.at[f])

    def part_copy(self, f, h):
        rows = pl.ds((h - 1) * VPAD, 2 * VPAD)
        return pltpu.make_async_copy(self.acc.at[f, rows], self.state_out.at[f, rows], self.out_sem.at[f])

    def make_keys(self, seg):
        self.k[0:seg.shape[1], :] = tn(seg, self.wkp[...]).astype(BF16)

    def make_values(self, seg):
        keys = seg.shape[1]
        ones_row = lax.broadcasted_iota(I32, (16, keys), 0) == self.dim % 16
        vt = dot(self.wvt[...], seg).astype(BF16)
        for h in range(HEADS):
            at, end = h * VPAD + self.dim // 16 * 16, (h + 1) * VPAD
            self.vt[h * VPAD:at, 0:keys] = vt[h * VPAD:at]
            self.vt[at:at + 16, 0:keys] = jnp.where(ones_row, jnp.ones((16, keys), BF16), vt[at:at + 16])
            if at + 16 < end:
                self.vt[at + 16:end, 0:keys] = vt[at + 16:end]

    def scores(self, f, h, keys):
        own = self.qt[f, h * KPAD:(h + 1) * KPAD, :]
        zeros = jnp.zeros((KPAD, self.tok), BF16)
        both = jnp.concatenate([own, zeros] if h % 2 == 0 else [zeros, own], axis=0)
        lanes = h // 2 * 2 * KPAD
        self.s[h % 2, 0:keys] = dot(self.k[0:keys, lanes:lanes + 2 * KPAD], both)

    def begin(self, f, seg):
        self.make_keys(seg)
        self.make_values(seg)
        self.scores(f, 0, seg.shape[1])

    def item(self, f, keys, after=None, seg=None, first=False, attended=None, leave=False):
        for h in range(HEADS):
            top = jnp.max(self.s[h % 2, 0:keys], axis=0, keepdims=True)
            if h + 1 < HEADS:
                self.scores(f, h + 1, keys)
            elif after is not None:
                if seg is not None:
                    self.make_keys(seg)
                self.scores(after, 0, keys if seg is None else seg.shape[1])
            rows = slice(h * VPAD, (h + 1) * VPAD)
            if not first:
                kept = self.acc[f, rows, :]
                old = kept[self.dim + 1:self.dim + 2]
                top = jnp.maximum(top, old)
            weights = jnp.exp2((self.s[h % 2, 0:keys] - top) * self.factor).astype(BF16)
            part = dot(self.vt[rows, 0:keys], weights)
            if not first:
                part = part + kept * jnp.exp2((old - top) * self.factor)
            if attended is not None:
                attended[rows, :] = (part / part[self.dim:self.dim + 1]).astype(BF16)
            else:
                self.acc[f, rows, :] = part
                self.acc[f, h * VPAD + self.dim + 1:h * VPAD + self.dim + 2, :] = top
                if leave and h % 2 == 1:
                    self.part_copy(f, h).start()
        if after is not None and seg is not None:
            self.make_values(seg)


class Arriving:
    def __init__(self, hbm, near_ref, sem, start=0):
        self.hbm, self.near, self.sem = hbm, near_ref, sem
        for k in range(start, hbm.shape[0]):
            self.copy(k).start()

    def copy(self, k):
        return pltpu.make_async_copy(self.hbm.at[k], self.near.at[k], self.sem.at[k])

    def __getitem__(self, k):
        self.copy(k).wait()
        return self.near[k]


def own_kernel(qt_ref, wkp_ref, wvt_ref, first_ref, main_hbm, state_out, main_near, main_sem, *scratch):
    flash = Flash(qt_ref, wkp_ref, wvt_ref, None, state_out, scratch)
    frames, keys = qt_ref.shape[0], main_hbm.shape[2]
    main = Arriving(main_hbm, main_near, main_sem, 1)
    flash.begin(1, first_ref[0])

    @pl.loop(1, frames - 1)
    def _(f):
        flash.item(f, keys, f + 1, main[f], first=True)
        flash.out_copy(f).start()

    flash.item(frames - 1, keys, first=True, leave=True)
    for f in range(1, frames):
        flash.out_copy(f).wait()


def side_kernel(qt_ref, wkp_ref, wvt_ref, prev_ref, first_ref, side_hbm, state_in, state_out, mirror_ref,
                side_near, side_sem, *scratch):
    flash = Flash(qt_ref, wkp_ref, wvt_ref, state_in, state_out, scratch)
    frames, keys = qt_ref.shape[0], side_hbm.shape[2]
    side = Arriving(side_hbm, side_near, side_sem)
    for f in range(1, frames):
        flash.in_copy(f).start()
    flash.begin(0, jnp.where(lax.axis_index("frame") > 0, prev_ref[0], first_ref[0]))
    leading = side[0]
    mirror_ref[0] = leading
    flash.item(0, prev_ref.shape[2], 1, leading, first=True)
    flash.out_copy(0).start()

    @pl.loop(1, frames - 1)
    def _(f):
        flash.in_copy(f).wait()
        flash.item(f, keys, f + 1, side[f])
        flash.out_copy(f).start()

    flash.in_copy(frames - 1).wait()
    flash.item(frames - 1, keys, leave=True)
    for f in range(frames):
        flash.out_copy(f).wait()


def lead_kernel(qt_ref, wkp_ref, wvt_ref, prev_ref, mirror_ref, lead_ref, state_in, state_out, *scratch):
    flash = Flash(qt_ref, wkp_ref, wvt_ref, state_in, state_out, scratch)
    frames, keys = qt_ref.shape[0], lead_ref.shape[2]
    for f in range(frames):
        flash.in_copy(f).start()
    flash.begin(0, jnp.where(lax.axis_index("frame") > 0, prev_ref[0], mirror_ref[0]))
    flash.in_copy(0).wait()
    flash.item(0, prev_ref.shape[2], 0, lead_ref[0])
    flash.item(0, keys, 1)
    flash.out_copy(0).start()

    @pl.loop(1, frames - 1)
    def _(f):
        flash.in_copy(f).wait()
        flash.item(f, keys, f + 1)
        flash.out_copy(f).start()

    flash.in_copy(frames - 1).wait()
    flash.item(frames - 1, keys, leave=True)
    for f in range(frames):
        flash.out_copy(f).wait()


def finish_kernel(start, rows, pair, fresh, *refs):
    refs = list(refs)
    take = lambda n: [refs.pop(0) for _ in range(n)]
    qt_ref, wkp_ref, wvt_ref, wop_ref = take(4)
    if fresh:
        (seg_ref,) = take(1)
    else:
        k_ref, vt_ref = take(2)
    state_hbm, x_hbm, upd_ref, edge_ref, stat_ref = take(5)
    if fresh:
        k_ref, vt_ref = take(2)
    att_ref, x_ref, x_sem = take(3)
    count, tok, ch = x_ref.shape
    cols, keys = tok // rows, k_ref.shape[0]
    flash = Flash(qt_ref, wkp_ref, wvt_ref, state_hbm, None, refs)
    flash.k, flash.vt = k_ref, vt_ref
    for f in range(start, start + count):
        flash.in_copy(f).start()
    copy = pltpu.make_async_copy(x_hbm.at[pl.ds(start, count)], x_ref, x_sem)
    copy.start()
    if fresh:
        flash.begin(start, seg_ref[0])
    else:
        flash.scores(start, 0, keys)

    @pl.loop(0, count)
    def _(i):
        flash.in_copy(start + i).wait()
        flash.item(start + i, keys, start + jnp.minimum(i + 1, count - 1), attended=att_ref)

        @pl.when(i == 0)
        def _():
            copy.wait()

        mixed = tn(att_ref[...], wop_ref[...])
        updated = (x_ref[i].astype(F32) + mixed).astype(BF16)
        upd_ref[i] = updated
        floated = updated.astype(F32)
        sums = jnp.sum(floated, axis=0, keepdims=True)
        squares = jnp.sum(floated * floated, axis=0, keepdims=True)
        which = lax.broadcasted_iota(I32, (8, ch), 0)
        stats = jnp.where(which == 0, sums, jnp.where(which == 1, squares, 0.0))
        stat_ref[i] = stats
        if pair:
            edge_ref[i, 0:cols] = jnp.where(lax.axis_index("row") == 0, floated[tok - cols:], floated[:cols])
            edge_ref[i, cols:cols + 8] = stats
        else:
            edge_ref[i, 0:cols] = floated[:cols]
            edge_ref[i, cols:2 * cols] = floated[tok - cols:]


def flash_scratch(qt, keys, held=True):
    frames, nk, tok = qt.shape
    nv = HEADS * VPAD
    out = [pltpu.VMEM((frames, nv, tok), F32), pltpu.VMEM((2, keys, tok), F32)]
    out += [pltpu.SemaphoreType.DMA((frames,))] * 2
    return out + ([pltpu.VMEM((keys, nk), BF16), pltpu.VMEM((nv, keys), BF16)] if held else [])


def flash_cost(items, keys, tok):
    made = items * HEADS * keys * tok
    return cost(made * 140, made // 80, made // 10)


def flash(body, name, qt, wkp, wvt, segments, state, items, moved=None, mirrored=False):
    frames, _, tok = qt.shape
    keys = max(s.shape[2] for s in segments + ([] if moved is None else [moved]))
    near_args, far_args, scratch = [qt, wkp, wvt] + segments, [], []
    if moved is not None:
        far_args.append(moved)
        scratch = [pltpu.VMEM(moved.shape, BF16), pltpu.SemaphoreType.DMA((moved.shape[0],))]
    aliases = {}
    if state is not None:
        far_args.append(state)
        aliases = {len(near_args) + len(far_args) - 1: 0}
    outs = [far_of(frames, HEADS * VPAD, tok, dtype=F32)] + ([near_of(1, *moved.shape[1:])] if mirrored else [])
    got = kernel_call(body, name, near_args, far_args, outs, scratch + flash_scratch(qt, keys),
                      flash_cost(items, keys, tok), aliases)
    return got if mirrored else got[0]


def finish(start, count, qt, wkp, wvt, wop, state, lead_side, made, x, rows, pair):
    tok, ch = x.shape[1:]
    cols, nk, nv, keys = tok // rows, HEADS * KPAD, HEADS * VPAD, lead_side.shape[2]
    fresh = made is None
    outs = [near_of(count, tok, ch), near_of(count, cols + 8 if pair else 2 * cols, ch, dtype=F32),
            near_of(count, 8, ch, dtype=F32)]
    if fresh:
        outs += [near_of(keys, nk), near_of(nv, keys)]
    scratch = [pltpu.VMEM((nv, tok), BF16), pltpu.VMEM((count, tok, ch), BF16), pltpu.SemaphoreType.DMA]
    got = kernel_call(functools.partial(finish_kernel, start, rows, pair, fresh), "finish",
                      [qt, wkp, wvt, wop] + ([lead_side] if fresh else list(made)), [state, x], outs,
                      scratch + flash_scratch(qt, keys, held=False), flash_cost(count, keys, tok))
    return got[:3], (tuple(got[3:]) if fresh else made)


def conv_kernel(start, rows, counted, pair, fresh, *refs):
    refs = list(refs)
    take = lambda n: [refs.pop(0) for _ in range(n)]
    upd_ref, top_ref, bot_ref, stat_ref, gn_ref, bias_ref, w_ref = take(7)
    if not fresh:
        take(1)
    (out_hbm,) = take(1)
    if fresh:
        (wide_ref,) = take(1)
    act_ref, out_ref, sems = refs
    count, tok, ch = upd_ref.shape
    cols = tok // rows
    if fresh:
        for a in range(3):
            for b in range(3):
                wide_ref[a * ch:(a + 1) * ch, b * ch:(b + 1) * ch] = w_ref[a, b]
    else:
        wide_ref = w_ref

    stats = jnp.concatenate([stat_ref[i] + top_ref[i, cols:cols + 8] if pair else stat_ref[i]
                             for i in range(count)], axis=0)
    width = ch // GROUPS
    first = lax.broadcasted_iota(I32, (ch, ch), 0)
    second = lax.broadcasted_iota(I32, (ch, ch), 1)
    group_of = lambda v: (v * (65536 // width + 1)) >> 16
    same = jnp.where(group_of(first) == group_of(second), 1.0, 0.0).astype(BF16)
    high = stats.astype(BF16)
    rest = stats - high.astype(F32)
    middle = rest.astype(BF16)
    low = (rest - middle.astype(F32)).astype(BF16)
    grouped = (dot(high, same) + dot(middle, same) + dot(low, same)) / counted
    gain = gn_ref[...].astype(F32).reshape(1, ch)
    bias = bias_ref[...].astype(F32).reshape(1, ch)
    me = lax.axis_index("row")
    column = lax.broadcasted_iota(I32, (tok, ch), 0) % cols
    copies = []
    for i in range(count):
        mean = grouped[8 * i:8 * i + 1]
        scale = lax.rsqrt(grouped[8 * i + 1:8 * i + 2] - mean * mean + 1e-05) * gain

        def activated(u):
            v = (u.astype(F32) - mean) * scale
            return (v / (1.0 + jnp.exp(-v))).astype(BF16)

        above = jnp.where(me > 0, activated(top_ref[i, 0:cols]), jnp.zeros((cols, ch), BF16))
        below = jnp.where(me < lax.axis_size("row") - 1, activated(bot_ref[i, 0:cols]), jnp.zeros((cols, ch), BF16))
        inner = activated(upd_ref[i])
        act_ref[:, ch:2 * ch] = inner
        act_ref[0:cols, 0:ch] = above
        act_ref[cols:tok, 0:ch] = inner[0:tok - cols]
        act_ref[0:tok - cols, 2 * ch:] = inner[cols:tok]
        act_ref[tok - cols:tok, 2 * ch:] = below
        parts = dot(act_ref[...], wide_ref[...])
        left = jnp.where(column == 0, 0.0, pltpu.roll(parts[:, 0:ch], 1, 0))
        right = jnp.where(column == cols - 1, 0.0, pltpu.roll(parts[:, 2 * ch:], tok - 1, 0))
        out_ref[i] = (upd_ref[i].astype(F32) + (left + parts[:, ch:2 * ch] + right) + bias).astype(BF16)
        copies.append(pltpu.make_async_copy(out_ref.at[i], out_hbm.at[start + i], sems.at[i]))
        copies[-1].start()
    for copy in copies:
        copy.wait()


def conv(start, frames, upd, top, bot, stats, gn, bias, weight, rows, pair, counted, into=None):
    count, tok, ch = upd.shape
    fresh = into is None
    args = [upd, top, bot, stats, gn, bias, weight if fresh else into[1]]
    outs = [far_of(frames, tok, ch)] + ([near_of(3 * ch, 3 * ch)] if fresh else [])
    scratch = [pltpu.VMEM((tok, 3 * ch), BF16), pltpu.VMEM((count, tok, ch), BF16),
               pltpu.SemaphoreType.DMA((count,))]
    got = kernel_call(functools.partial(conv_kernel, start, rows, counted, pair, fresh), "conv",
                      args, [] if fresh else [into[0]], outs, scratch, cost(count * tok * ch * ch * 30, 4e6),
                      {} if fresh else {len(args): 0})
    return got[0], got[1] if fresh else into[1]


def fan(value, axis, heads, steps):
    size = lax.axis_size(axis)
    got = {}
    for k in steps:
        route = [(i, i + k) for i in heads if i + k < size]
        if route:
            got[k] = lax.ppermute(value, axis, route)
    return got


def chosen_kernel(axis, modulus, places, *refs):
    place = lax.axis_index(axis) % modulus
    *sources, out_hbm, sem = refs
    elsewhere = place >= 0
    for k, source in zip(places, sources[1:]):
        here = place == k
        elsewhere = elsewhere & (place != k)

        @pl.when(here)
        def _(source=source):
            copy = pltpu.make_async_copy(source, out_hbm, sem)
            copy.start()
            copy.wait()

    @pl.when(elsewhere)
    def _():
        copy = pltpu.make_async_copy(sources[0], out_hbm, sem)
        copy.start()
        copy.wait()


def chosen(value, axis, got, modulus):
    anywhere = pl.BlockSpec(memory_space=pl.ANY)
    return pl.pallas_call(
        functools.partial(chosen_kernel, axis, modulus, tuple(got)),
        in_specs=[anywhere] * (1 + len(got)),
        out_specs=anywhere,
        out_shape=jax.ShapeDtypeStruct(value.shape, value.dtype),
        scratch_shapes=[pltpu.SemaphoreType.DMA],
        compiler_params=pltpu.CompilerParams(vmem_limit_bytes=VMEM_BYTES),
        cost_estimate=cost(0, 2 * value.size),
        name="chosen",
    )(value, *got.values())


def others(value, rows):
    got = [lax.ppermute(value, "row", [(i, (i + k) % rows) for i in range(rows)]) for k in range(1, rows)]
    return got[0] if len(got) == 1 else jnp.concatenate(got, axis=2)


def body(latents, ln_gain, q_weight, k_weight, v_weight, o_weight, gn_gain, conv_weight, conv_bias):
    frames, row_count, cols, ch = latents.shape
    tok = row_count * cols
    size, blocks = lax.axis_size("row"), lax.axis_size("frame")
    pair = size == 2
    x = latents.reshape(frames, tok, ch)

    qt, main, lead, tail, wkp, wvt, wop = project(x, ln_gain, q_weight, k_weight, v_weight, o_weight)
    common = (qt, wkp, wvt)
    routes = [[(f * size + r, (f + 1) * size + (r + k) % size) for f in range(blocks - 1) for r in range(size)]
              for k in range(size)]
    inner = 1
    while inner * inner < blocks:
        inner *= 2
    side = others(main, size)
    prev = lax.ppermute(tail, ("frame", "row"), routes[0])
    spread = fan(lead, "frame", [0], range(inner, blocks, inner))
    first = lead
    state = flash(own_kernel, "own", *common, [first], None, frames - 1, moved=main)

    state, spread = lax.optimization_barrier((state, spread))
    side, tail = lax.optimization_barrier((side, tail))
    came = [lax.ppermute(tail, ("frame", "row"), route) for route in routes[1:]]
    prev_side = came[0] if pair else jnp.concatenate(came, axis=2)
    lead = chosen(lead, "frame", spread, blocks)
    spread = fan(lead, "frame", range(0, blocks, inner), range(1, inner))
    state, mirror = flash(side_kernel, "side", *common, [prev, first], state, frames, moved=side, mirrored=True)

    state, spread = lax.optimization_barrier((state, spread))
    lead = chosen(lead, "frame", spread, inner)
    lead_side = others(lead, size)
    state = flash(lead_kernel, "lead", *common, [prev_side, mirror, lead], state, frames + 1)

    half = frames // 2
    made, into, finished = None, None, []
    for start, count in ((0, half), (half, frames - half)):
        (upd, edge, stats), made = finish(start, count, *common, wop, state, lead_side, made, x, row_count, pair)
        if pair:
            top = bot = lax.ppermute(edge, "row", [(0, 1), (1, 0)])
        else:
            top = lax.ppermute(edge[:, cols:], "row", [(i, i + 1) for i in range(size - 1)])
            bot = lax.ppermute(edge[:, :cols], "row", [(i + 1, i) for i in range(size - 1)])
            stats = lax.psum(stats, "row")
        finished.append((start, upd, top, bot, stats))
    for start, upd, top, bot, stats in finished:
        into = conv(start, frames, upd, top, bot, stats, gn_gain, conv_bias, conv_weight,
                    row_count, pair, tok * size * (ch // GROUPS), into)
    return into[0].reshape(latents.shape)


def solution(mesh):
    in_specs = (P("frame", "row", None, None), P(), P(), P(), P(), P(), P(), P(), P())
    out_specs = P("frame", "row", None, None)
    return jax.shard_map(body, mesh=mesh, in_specs=in_specs, out_specs=out_specs, check_vma=False)
```

```python
import functools
import math

import jax
import jax.numpy as jnp
from jax import lax
from jax.experimental import pallas as pl
from jax.experimental.pallas import tpu as pltpu
from jax.sharding import PartitionSpec as P

HEADS = 8
GROUPS = 32
KPAD = 64
VPAD = 48
BF16, F32, I32 = jnp.bfloat16, jnp.float32, jnp.int32
VMEM_BYTES = 24 * 2**20
LOW = -1e30


def dot(a, b):
    return jnp.dot(a, b, preferred_element_type=F32)


def nt(a, b):
    return lax.dot_general(a, b, (((1,), (1,)), ((), ())), preferred_element_type=F32)


def tn(a, b):
    return lax.dot_general(a, b, (((0,), (0,)), ((), ())), preferred_element_type=F32)


def cost(flops, moved, exps=0):
    return pl.CostEstimate(flops=int(flops), bytes_accessed=int(moved), transcendentals=int(exps))


def near_of(*dims, dtype=BF16):
    return pltpu.VMEM(dims, dtype)


def far_of(*dims, dtype=BF16):
    return pltpu.HBM(dims, dtype)


def near(a):
    return pltpu.with_memory_space_constraint(a, pltpu.VMEM)


def far(a):
    return pltpu.with_memory_space_constraint(a, pltpu.HBM)


def kernel_call(body, name, near_args, far_args, outs, scratch, price, aliases=None):
    in_vmem, anywhere = pl.BlockSpec(memory_space=pltpu.VMEM), pl.BlockSpec(memory_space=pl.ANY)
    return pl.pallas_call(
        body,
        in_specs=[in_vmem] * len(near_args) + [anywhere] * len(far_args),
        out_specs=[in_vmem if o.memory_space == pltpu.VMEM else anywhere for o in outs],
        out_shape=outs,
        scratch_shapes=scratch,
        input_output_aliases=aliases or {},
        compiler_params=pltpu.CompilerParams(vmem_limit_bytes=VMEM_BYTES),
        cost_estimate=price,
        name=name,
    )(*[near(a) for a in near_args], *[far(a) for a in far_args])


def head_spread(channels, pad):
    dim = channels // HEADS
    shape = (HEADS * pad, channels)
    row = lax.broadcasted_iota(I32, shape, 0)
    col = lax.broadcasted_iota(I32, shape, 1)
    head = sum((row >= h * pad).astype(I32) for h in range(1, HEADS))
    inside = row - head * pad
    return jnp.where((inside < dim) & (head * dim + inside == col), 1.0, 0.0).astype(BF16)


def norm_kernel(x_hbm, g_hbm, wq_hbm, wk_hbm, wv_hbm, wo_hbm, main_hbm, first_ref, last_ref, w_ref,
                x_ref, g_ref, main_ref, x_sem, g_sem, main_sem, w_sem):
    frames, tok, ch = x_ref.shape
    fetch_gain = pltpu.make_async_copy(g_hbm, g_ref, g_sem)
    fetch_gain.start()
    copies = [pltpu.make_async_copy(x_hbm.at[f], x_ref.at[f], x_sem.at[f]) for f in range(frames)]
    weights = [pltpu.make_async_copy(w, w_ref.at[k], w_sem.at[k])
               for k, w in enumerate((wq_hbm, wk_hbm, wv_hbm, wo_hbm))]
    for copy in copies + weights:
        copy.start()
    fetch_gain.wait()
    gain = jnp.broadcast_to(g_ref[...].astype(F32).reshape(1, ch), (8, ch)).T[:, 0:1]
    leave = []
    for f in range(frames):
        copies[f].wait()
        floated = x_ref[f].astype(F32).T
        centre = floated - jnp.sum(floated, axis=0, keepdims=True) / ch
        spread = jnp.sum(centre * centre, axis=0, keepdims=True) / ch
        value = (centre * lax.rsqrt(spread + 1e-05) * gain).astype(BF16)
        if f < frames - 1:
            main_ref[f] = value
            leave.append(pltpu.make_async_copy(main_ref.at[f], main_hbm.at[f], main_sem.at[f]))
            leave[-1].start()
        else:
            last_ref[0] = value
        if f == 0:
            first_ref[0] = value
    for copy in leave + weights:
        copy.wait()


def norm(x, gain, wq, wk, wv, wo):
    frames, tok, ch = x.shape
    outs = [far_of(frames - 1, ch, tok), near_of(1, ch, tok), near_of(1, ch, tok), near_of(4, ch, ch)]
    scratch = [pltpu.VMEM(x.shape, BF16), pltpu.VMEM((ch,), BF16), pltpu.VMEM((frames - 1, ch, tok), BF16),
               pltpu.SemaphoreType.DMA((frames,)), pltpu.SemaphoreType.DMA, pltpu.SemaphoreType.DMA((frames - 1,)),
               pltpu.SemaphoreType.DMA((4,))]
    return kernel_call(norm_kernel, "norm", [], [x, gain, wq, wk, wv, wo], outs, scratch, cost(frames * tok * ch * 20, 4e5))


def project_kernel(first_ref, last_ref, w_ref, main_hbm,
                   qt_ref, wkp_ref, wvt_ref, wop_ref, main_ref, main_sem):
    frames, ch = qt_ref.shape[0], first_ref.shape[1]
    blocks = [pltpu.make_async_copy(main_hbm.at[f], main_ref.at[f], main_sem.at[f]) for f in range(1, frames - 1)]
    for copy in blocks:
        copy.start()
    ek, ev = head_spread(ch, KPAD), head_spread(ch, VPAD)
    wqt = nt(ek, w_ref[0]).astype(BF16)
    wkp_ref[...] = nt(w_ref[1], ek).astype(BF16)
    wvt_ref[...] = nt(ev, w_ref[2]).astype(BF16)
    wop_ref[...] = dot(ev, w_ref[3]).astype(BF16)
    for copy in blocks:
        copy.wait()
    for f in range(frames):
        value = first_ref[0] if f == 0 else last_ref[0] if f == frames - 1 else main_ref[f]
        qt_ref[f] = dot(wqt, value).astype(BF16)


def project(main, first, last, weights):
    ch, tok = main.shape[1:]
    frames, nk, nv = main.shape[0] + 1, HEADS * KPAD, HEADS * VPAD
    outs = [near_of(frames, nk, tok), near_of(ch, nk), near_of(nv, ch), near_of(nv, ch)]
    scratch = [pltpu.VMEM(main.shape, BF16), pltpu.SemaphoreType.DMA((frames - 1,))]
    return kernel_call(project_kernel, "project", [first, last, weights], [main], outs, scratch,
                       cost(frames * tok * ch * nk, 8e5))


class Flash:
    def __init__(self, qt_ref, wkp_ref, wvt_ref, state_in, state_out, scratch):
        self.qt, self.wkp, self.wvt = qt_ref, wkp_ref, wvt_ref
        self.state_in, self.state_out = state_in, state_out
        self.acc, self.s, self.in_sem, self.out_sem, *kept = scratch
        if kept:
            self.k, self.vt = kept
        self.tok = qt_ref.shape[2]
        self.dim = wkp_ref.shape[0] // HEADS
        self.factor = math.log2(math.e) / math.sqrt(self.dim)

    def in_copy(self, f):
        return pltpu.make_async_copy(self.state_in.at[f], self.acc.at[f], self.in_sem.at[f])

    def out_copy(self, f):
        return pltpu.make_async_copy(self.acc.at[f], self.state_out.at[f], self.out_sem.at[f])

    def part_copy(self, f, h):
        rows = pl.ds((h - 1) * VPAD, 2 * VPAD)
        return pltpu.make_async_copy(self.acc.at[f, rows], self.state_out.at[f, rows], self.out_sem.at[f])

    def make_keys(self, seg):
        self.k[0:seg.shape[1], :] = tn(seg, self.wkp[...]).astype(BF16)

    def make_values(self, seg):
        keys = seg.shape[1]
        ones_row = lax.broadcasted_iota(I32, (16, keys), 0) == self.dim % 16
        vt = dot(self.wvt[...], seg).astype(BF16)
        for h in range(HEADS):
            at, end = h * VPAD + self.dim // 16 * 16, (h + 1) * VPAD
            self.vt[h * VPAD:at, 0:keys] = vt[h * VPAD:at]
            self.vt[at:at + 16, 0:keys] = jnp.where(ones_row, jnp.ones((16, keys), BF16), vt[at:at + 16])
            if at + 16 < end:
                self.vt[at + 16:end, 0:keys] = vt[at + 16:end]

    def scores(self, f, h, keys):
        own = self.qt[f, h * KPAD:(h + 1) * KPAD, :]
        zeros = jnp.zeros((KPAD, self.tok), BF16)
        both = jnp.concatenate([own, zeros] if h % 2 == 0 else [zeros, own], axis=0)
        lanes = h // 2 * 2 * KPAD
        self.s[h % 2, 0:keys] = dot(self.k[0:keys, lanes:lanes + 2 * KPAD], both)

    def begin(self, f, seg):
        self.make_keys(seg)
        self.make_values(seg)
        self.scores(f, 0, seg.shape[1])

    def item(self, f, keys, after=None, seg=None, first=False, attended=None, leave=False):
        for h in range(HEADS):
            top = jnp.max(self.s[h % 2, 0:keys], axis=0, keepdims=True)
            if h + 1 < HEADS:
                self.scores(f, h + 1, keys)
            elif after is not None:
                if seg is not None:
                    self.make_keys(seg)
                self.scores(after, 0, keys if seg is None else seg.shape[1])
            rows = slice(h * VPAD, (h + 1) * VPAD)
            if not first:
                kept = self.acc[f, rows, :]
                old = kept[self.dim + 1:self.dim + 2]
                top = jnp.maximum(top, old)
            weights = jnp.exp2((self.s[h % 2, 0:keys] - top) * self.factor).astype(BF16)
            part = dot(self.vt[rows, 0:keys], weights)
            if not first:
                part = part + kept * jnp.exp2((old - top) * self.factor)
            if attended is not None:
                attended[rows, :] = (part / part[self.dim:self.dim + 1]).astype(BF16)
            else:
                self.acc[f, rows, :] = part
                self.acc[f, h * VPAD + self.dim + 1:h * VPAD + self.dim + 2, :] = top
                if leave and h % 2 == 1:
                    self.part_copy(f, h).start()
        if after is not None and seg is not None:
            self.make_values(seg)


class Arriving:
    def __init__(self, hbm, near_ref, sem, start=0):
        self.hbm, self.near, self.sem = hbm, near_ref, sem
        for k in range(start, hbm.shape[0]):
            self.copy(k).start()

    def copy(self, k):
        return pltpu.make_async_copy(self.hbm.at[k], self.near.at[k], self.sem.at[k])

    def __getitem__(self, k):
        self.copy(k).wait()
        return self.near[k]


def own_kernel(qt_ref, wkp_ref, wvt_ref, first_ref, main_hbm, state_out, main_near, main_sem, *scratch):
    flash = Flash(qt_ref, wkp_ref, wvt_ref, None, state_out, scratch)
    frames, keys = qt_ref.shape[0], main_hbm.shape[2]
    main = Arriving(main_hbm, main_near, main_sem, 1)
    flash.begin(1, first_ref[0])

    @pl.loop(1, frames - 1)
    def _(f):
        flash.item(f, keys, f + 1, main[f], first=True)
        flash.out_copy(f).start()

    flash.item(frames - 1, keys, first=True, leave=True)
    for f in range(1, frames):
        flash.out_copy(f).wait()


def side_kernel(qt_ref, wkp_ref, wvt_ref, prev_ref, first_ref, side_hbm, state_in, state_out, mirror_ref,
                side_near, side_sem, *scratch):
    flash = Flash(qt_ref, wkp_ref, wvt_ref, state_in, state_out, scratch)
    frames, keys = qt_ref.shape[0], side_hbm.shape[2]
    side = Arriving(side_hbm, side_near, side_sem)
    for f in range(1, frames):
        flash.in_copy(f).start()
    flash.begin(0, jnp.where(lax.axis_index("frame") > 0, prev_ref[0], first_ref[0]))
    leading = side[0]
    mirror_ref[0] = leading
    flash.item(0, prev_ref.shape[2], 1, leading, first=True)
    flash.out_copy(0).start()

    @pl.loop(1, frames - 1)
    def _(f):
        flash.in_copy(f).wait()
        flash.item(f, keys, f + 1, side[f])
        flash.out_copy(f).start()

    flash.in_copy(frames - 1).wait()
    flash.item(frames - 1, keys, leave=True)
    for f in range(frames):
        flash.out_copy(f).wait()


def lead_kernel(qt_ref, wkp_ref, wvt_ref, prev_ref, mirror_ref, lead_ref, state_in, state_out, *scratch):
    flash = Flash(qt_ref, wkp_ref, wvt_ref, state_in, state_out, scratch)
    frames, keys = qt_ref.shape[0], lead_ref.shape[2]
    for f in range(frames):
        flash.in_copy(f).start()
    flash.begin(0, jnp.where(lax.axis_index("frame") > 0, prev_ref[0], mirror_ref[0]))
    flash.in_copy(0).wait()
    flash.item(0, prev_ref.shape[2], 0, lead_ref[0])
    flash.item(0, keys, 1)
    flash.out_copy(0).start()

    @pl.loop(1, frames - 1)
    def _(f):
        flash.in_copy(f).wait()
        flash.item(f, keys, f + 1)
        flash.out_copy(f).start()

    flash.in_copy(frames - 1).wait()
    flash.item(frames - 1, keys, leave=True)
    for f in range(frames):
        flash.out_copy(f).wait()


def finish_kernel(start, rows, pair, fresh, *refs):
    refs = list(refs)
    take = lambda n: [refs.pop(0) for _ in range(n)]
    qt_ref, wkp_ref, wvt_ref, wop_ref = take(4)
    if fresh:
        (seg_ref,) = take(1)
    else:
        k_ref, vt_ref = take(2)
    state_hbm, x_hbm, upd_ref, edge_ref, stat_ref = take(5)
    if fresh:
        k_ref, vt_ref = take(2)
    att_ref, x_ref, x_sem = take(3)
    count, tok, ch = x_ref.shape
    cols, keys = tok // rows, k_ref.shape[0]
    flash = Flash(qt_ref, wkp_ref, wvt_ref, state_hbm, None, refs)
    flash.k, flash.vt = k_ref, vt_ref
    for f in range(start, start + count):
        flash.in_copy(f).start()
    copy = pltpu.make_async_copy(x_hbm.at[pl.ds(start, count)], x_ref, x_sem)
    copy.start()
    if fresh:
        flash.begin(start, seg_ref[0])
    else:
        flash.scores(start, 0, keys)

    @pl.loop(0, count)
    def _(i):
        flash.in_copy(start + i).wait()
        flash.item(start + i, keys, start + jnp.minimum(i + 1, count - 1), attended=att_ref)

        @pl.when(i == 0)
        def _():
            copy.wait()

        mixed = tn(att_ref[...], wop_ref[...])
        updated = (x_ref[i].astype(F32) + mixed).astype(BF16)
        upd_ref[i] = updated
        floated = updated.astype(F32)
        sums = jnp.sum(floated, axis=0, keepdims=True)
        squares = jnp.sum(floated * floated, axis=0, keepdims=True)
        which = lax.broadcasted_iota(I32, (8, ch), 0)
        stats = jnp.where(which == 0, sums, jnp.where(which == 1, squares, 0.0))
        stat_ref[i] = stats
        if pair:
            edge_ref[i, 0:cols] = jnp.where(lax.axis_index("row") == 0, floated[tok - cols:], floated[:cols])
            edge_ref[i, cols:cols + 8] = stats
        else:
            edge_ref[i, 0:cols] = floated[:cols]
            edge_ref[i, cols:2 * cols] = floated[tok - cols:]


def flash_scratch(qt, keys, held=True):
    frames, nk, tok = qt.shape
    nv = HEADS * VPAD
    out = [pltpu.VMEM((frames, nv, tok), F32), pltpu.VMEM((2, keys, tok), F32)]
    out += [pltpu.SemaphoreType.DMA((frames,))] * 2
    return out + ([pltpu.VMEM((keys, nk), BF16), pltpu.VMEM((nv, keys), BF16)] if held else [])


def flash_cost(items, keys, tok):
    made = items * HEADS * keys * tok
    return cost(made * 140, made // 80, made // 10)


def flash(body, name, qt, wkp, wvt, segments, state, items, moved=None, mirrored=False):
    frames, _, tok = qt.shape
    keys = max(s.shape[2] for s in segments + ([] if moved is None else [moved]))
    near_args, far_args, scratch = [qt, wkp, wvt] + segments, [], []
    if moved is not None:
        far_args.append(moved)
        scratch = [pltpu.VMEM(moved.shape, BF16), pltpu.SemaphoreType.DMA((moved.shape[0],))]
    aliases = {}
    if state is not None:
        far_args.append(state)
        aliases = {len(near_args) + len(far_args) - 1: 0}
    outs = [far_of(frames, HEADS * VPAD, tok, dtype=F32)] + ([near_of(1, *moved.shape[1:])] if mirrored else [])
    got = kernel_call(body, name, near_args, far_args, outs, scratch + flash_scratch(qt, keys),
                      flash_cost(items, keys, tok), aliases)
    return got if mirrored else got[0]


def finish(start, count, qt, wkp, wvt, wop, state, lead_side, made, x, rows, pair):
    tok, ch = x.shape[1:]
    cols, nk, nv, keys = tok // rows, HEADS * KPAD, HEADS * VPAD, lead_side.shape[2]
    fresh = made is None
    outs = [near_of(count, tok, ch), near_of(count, cols + 8 if pair else 2 * cols, ch, dtype=F32),
            near_of(count, 8, ch, dtype=F32)]
    if fresh:
        outs += [near_of(keys, nk), near_of(nv, keys)]
    scratch = [pltpu.VMEM((nv, tok), BF16), pltpu.VMEM((count, tok, ch), BF16), pltpu.SemaphoreType.DMA]
    got = kernel_call(functools.partial(finish_kernel, start, rows, pair, fresh), "finish",
                      [qt, wkp, wvt, wop] + ([lead_side] if fresh else list(made)), [state, x], outs,
                      scratch + flash_scratch(qt, keys, held=False), flash_cost(count, keys, tok))
    return got[:3], (tuple(got[3:]) if fresh else made)


def conv_kernel(start, rows, counted, pair, fresh, *refs):
    refs = list(refs)
    take = lambda n: [refs.pop(0) for _ in range(n)]
    upd_ref, top_ref, bot_ref, stat_ref, gn_ref, bias_ref, w_ref = take(7)
    if not fresh:
        take(1)
    (out_hbm,) = take(1)
    if fresh:
        (wide_ref,) = take(1)
    act_ref, out_ref, sems = refs
    count, tok, ch = upd_ref.shape
    cols = tok // rows
    if fresh:
        for a in range(3):
            for b in range(3):
                wide_ref[a * ch:(a + 1) * ch, b * ch:(b + 1) * ch] = w_ref[a, b]
    else:
        wide_ref = w_ref

    stats = jnp.concatenate([stat_ref[i] + top_ref[i, cols:cols + 8] if pair else stat_ref[i]
                             for i in range(count)], axis=0)
    width = ch // GROUPS
    first = lax.broadcasted_iota(I32, (ch, ch), 0)
    second = lax.broadcasted_iota(I32, (ch, ch), 1)
    group_of = lambda v: (v * (65536 // width + 1)) >> 16
    same = jnp.where(group_of(first) == group_of(second), 1.0, 0.0).astype(BF16)
    high = stats.astype(BF16)
    rest = stats - high.astype(F32)
    middle = rest.astype(BF16)
    low = (rest - middle.astype(F32)).astype(BF16)
    grouped = (dot(high, same) + dot(middle, same) + dot(low, same)) / counted
    gain = gn_ref[...].astype(F32).reshape(1, ch)
    bias = bias_ref[...].astype(F32).reshape(1, ch)
    me = lax.axis_index("row")
    column = lax.broadcasted_iota(I32, (tok, ch), 0) % cols
    copies = []
    for i in range(count):
        mean = grouped[8 * i:8 * i + 1]
        scale = lax.rsqrt(grouped[8 * i + 1:8 * i + 2] - mean * mean + 1e-05) * gain

        def activated(u):
            v = (u.astype(F32) - mean) * scale
            return (v / (1.0 + jnp.exp(-v))).astype(BF16)

        above = jnp.where(me > 0, activated(top_ref[i, 0:cols]), jnp.zeros((cols, ch), BF16))
        below = jnp.where(me < lax.axis_size("row") - 1, activated(bot_ref[i, 0:cols]), jnp.zeros((cols, ch), BF16))
        inner = activated(upd_ref[i])
        act_ref[:, ch:2 * ch] = inner
        act_ref[0:cols, 0:ch] = above
        act_ref[cols:tok, 0:ch] = inner[0:tok - cols]
        act_ref[0:tok - cols, 2 * ch:] = inner[cols:tok]
        act_ref[tok - cols:tok, 2 * ch:] = below
        parts = dot(act_ref[...], wide_ref[...])
        left = jnp.where(column == 0, 0.0, pltpu.roll(parts[:, 0:ch], 1, 0))
        right = jnp.where(column == cols - 1, 0.0, pltpu.roll(parts[:, 2 * ch:], tok - 1, 0))
        out_ref[i] = (upd_ref[i].astype(F32) + (left + parts[:, ch:2 * ch] + right) + bias).astype(BF16)
        copies.append(pltpu.make_async_copy(out_ref.at[i], out_hbm.at[start + i], sems.at[i]))
        copies[-1].start()
    for copy in copies:
        copy.wait()


def conv(start, frames, upd, top, bot, stats, gn, bias, weight, rows, pair, counted, into=None):
    count, tok, ch = upd.shape
    fresh = into is None
    args = [upd, top, bot, stats, gn, bias, weight if fresh else into[1]]
    outs = [far_of(frames, tok, ch)] + ([near_of(3 * ch, 3 * ch)] if fresh else [])
    scratch = [pltpu.VMEM((tok, 3 * ch), BF16), pltpu.VMEM((count, tok, ch), BF16),
               pltpu.SemaphoreType.DMA((count,))]
    got = kernel_call(functools.partial(conv_kernel, start, rows, counted, pair, fresh), "conv",
                      args, [] if fresh else [into[0]], outs, scratch, cost(count * tok * ch * ch * 30, 4e6),
                      {} if fresh else {len(args): 0})
    return got[0], got[1] if fresh else into[1]


def fan(value, axis, heads, steps):
    size = lax.axis_size(axis)
    got = {}
    for k in steps:
        route = [(i, i + k) for i in heads if i + k < size]
        if route:
            got[k] = lax.ppermute(value, axis, route)
    return got


def chosen_kernel(axis, modulus, places, *refs):
    place = lax.axis_index(axis) % modulus
    *sources, out_hbm, sem = refs
    elsewhere = place >= 0
    for k, source in zip(places, sources[1:]):
        here = place == k
        elsewhere = elsewhere & (place != k)

        @pl.when(here)
        def _(source=source):
            copy = pltpu.make_async_copy(source, out_hbm, sem)
            copy.start()
            copy.wait()

    @pl.when(elsewhere)
    def _():
        copy = pltpu.make_async_copy(sources[0], out_hbm, sem)
        copy.start()
        copy.wait()


def chosen(value, axis, got, modulus):
    anywhere = pl.BlockSpec(memory_space=pl.ANY)
    return pl.pallas_call(
        functools.partial(chosen_kernel, axis, modulus, tuple(got)),
        in_specs=[anywhere] * (1 + len(got)),
        out_specs=anywhere,
        out_shape=jax.ShapeDtypeStruct(value.shape, value.dtype),
        scratch_shapes=[pltpu.SemaphoreType.DMA],
        compiler_params=pltpu.CompilerParams(vmem_limit_bytes=VMEM_BYTES),
        cost_estimate=cost(0, 2 * value.size),
        name="chosen",
    )(value, *got.values())


def others(value, rows):
    got = [lax.ppermute(value, "row", [(i, (i + k) % rows) for i in range(rows)]) for k in range(1, rows)]
    return got[0] if len(got) == 1 else jnp.concatenate(got, axis=2)


def body(latents, ln_gain, q_weight, k_weight, v_weight, o_weight, gn_gain, conv_weight, conv_bias):
    frames, row_count, cols, ch = latents.shape
    tok = row_count * cols
    size, blocks = lax.axis_size("row"), lax.axis_size("frame")
    pair = size == 2
    x = latents.reshape(frames, tok, ch)

    main, lead, tail, weights = norm(x, ln_gain, q_weight, k_weight, v_weight, o_weight)
    qt, wkp, wvt, wop = project(main, lead, tail, weights)
    common = (qt, wkp, wvt)
    routes = [[(f * size + r, (f + 1) * size + (r + k) % size) for f in range(blocks - 1) for r in range(size)]
              for k in range(size)]
    inner = 1
    while inner * inner < blocks:
        inner *= 2
    side = others(main, size)
    prev = lax.ppermute(tail, ("frame", "row"), routes[0])
    spread = fan(lead, "frame", [0], range(inner, blocks, inner))
    first = lead
    state = flash(own_kernel, "own", *common, [first], None, frames - 1, moved=main)

    state, spread = lax.optimization_barrier((state, spread))
    side, tail = lax.optimization_barrier((side, tail))
    came = [lax.ppermute(tail, ("frame", "row"), route) for route in routes[1:]]
    prev_side = came[0] if pair else jnp.concatenate(came, axis=2)
    lead = chosen(lead, "frame", spread, blocks)
    spread = fan(lead, "frame", range(0, blocks, inner), range(1, inner))
    state, mirror = flash(side_kernel, "side", *common, [prev, first], state, frames, moved=side, mirrored=True)

    state, spread = lax.optimization_barrier((state, spread))
    lead = chosen(lead, "frame", spread, inner)
    lead_side = others(lead, size)
    state = flash(lead_kernel, "lead", *common, [prev_side, mirror, lead], state, frames + 1)

    half = frames // 2
    made, into, finished = None, None, []
    for start, count in ((0, half), (half, frames - half)):
        (upd, edge, stats), made = finish(start, count, *common, wop, state, lead_side, made, x, row_count, pair)
        if pair:
            top = bot = lax.ppermute(edge, "row", [(0, 1), (1, 0)])
        else:
            top = lax.ppermute(edge[:, cols:], "row", [(i, i + 1) for i in range(size - 1)])
            bot = lax.ppermute(edge[:, :cols], "row", [(i + 1, i) for i in range(size - 1)])
            stats = lax.psum(stats, "row")
        finished.append((start, upd, top, bot, stats))
    for start, upd, top, bot, stats in finished:
        into = conv(start, frames, upd, top, bot, stats, gn_gain, conv_bias, conv_weight,
                    row_count, pair, tok * size * (ch // GROUPS), into)
    return into[0].reshape(latents.shape)


def solution(mesh):
    in_specs = (P("frame", "row", None, None), P(), P(), P(), P(), P(), P(), P(), P())
    out_specs = P("frame", "row", None, None)
    return jax.shard_map(body, mesh=mesh, in_specs=in_specs, out_specs=out_specs, check_vma=False)
```
